256 devices in a mesh: clique: 4 (over x), group: 64 (over z, y, core).
Axes of the slice: x: 4, y: 4, z: 8, core: 2. Of those that a mesh axis runs over, the one named last changes fastest.
Arguments:
- hot_shard: bfloat16 [65536, 128], P('clique'), may hold values from -6 to 6
- cold_shard: bfloat16 [1048576, 128], P('group'), may hold values from -6 to 6
- hot_ids: int32 [256, 4, 512], P(('clique', 'group')), may hold values from 0 to 16383
- cold_ids: int32 [256, 64, 32], P(('clique', 'group')), may hold values from 0 to 16383
- cold_counts: int32 [256, 64], P(('clique', 'group')), may hold values from 16 to 32, as said below
- mid_self: int32 [256, 7680], P(('clique', 'group')), may hold values from 0 to 4095, as said below
- nbr1: int32 [256, 10, 7680], P(('clique', 'group')), may hold values from 0 to 4095, as said below
- nbr2: int32 [256, 15, 512], P(('clique', 'group')), may hold values from 0 to 7679
- labels: int32 [256, 512], P(('clique', 'group')), may hold values from 0 to 171
- w1_self: bfloat16 [128, 256], replicated, may hold values from -0.5 to 0.5
- w1_neigh: bfloat16 [128, 256], replicated, may hold values from -0.5 to 0.5
- w2_self: bfloat16 [256, 172], replicated, may hold values from -1.5 to 1.5
- w2_neigh: bfloat16 [256, 172], replicated, may hold values from -1.5 to 1.5
Outputs:
- seed_loss: float32 [256, 512], P(('clique', 'group'))
- grad_w1_self: float32 [128, 256], replicated
- grad_w1_neigh: float32 [128, 256], replicated
- grad_w2_self: float32 [256, 172], replicated
- grad_w2_neigh: float32 [256, 172], replicated
The draws below stay inside these ranges and needn't reach their ends.
Inputs may be any that keep to these rules, and one draw needn't show every extreme that they name: `cold_counts`: the last store device has 32 live slots from every trainer; the other counts vary from store device to store device. `mid_self`: each entry is a position in the trainer's inputs that holds a hot row or a live cold slot. `nbr1`: each entry is a position in the trainer's inputs that holds a hot row or a live cold slot.
All inputs are finite; a program needn't handle non-finite values.
Results may differ from the reference program's by a relative error of at most 0.0021.
Values may be sent and summed in bfloat16 or wider, within the bound.
No kernel may reach another device: no remote copies, remote signals or barrier semaphores. Data moves between devices by JAX's collectives and lax.ppermute only.
A program may use at most 128 MiB of HBM per device.

```python
from functools import partial
import jax
import jax.numpy as jnp
from jax import lax

F = 128
HID = 256
CLASSES = 172
FAN0 = 10
FAN1 = 15
SEEDS = 512
HOT_ROWS = 2048
COLD_ROWS = 2048
HOT_SHARD = 16384
COLD_SHARD = 16384
MID = 7680
HOT_SLOT = 512
COLD_SLOT = 32
HOT_TABLE = 65536
COLD_TABLE = 1048576
N_CLIQUE = 4
N_GROUP = 64
DEVICES = 256


def shared_counts(key):
    key = jax.random.fold_in(key, 101)
    second, third = jax.random.split(key, 2)
    weights = jax.random.randint(second, (N_GROUP,), 1, 4)
    raw_counts = jax.random.randint(third, (DEVICES, N_GROUP), COLD_SLOT // 2, COLD_SLOT + 1)
    counts = jnp.minimum(raw_counts * weights[None, :], COLD_SLOT)
    owners = jnp.arange(N_GROUP, dtype=jnp.int32)[None, :]
    return jnp.where(owners == N_GROUP - 1, COLD_SLOT, counts).astype(jnp.int32)


def live_positions(key, counts, tail):
    totals = HOT_ROWS + jnp.sum(counts, axis=1)

    def one_trainer(subkey, row_counts, row_total):
        picks = jax.random.randint(subkey, tail, 0, row_total)
        bounds = jnp.cumsum(row_counts)
        offset = picks - HOT_ROWS
        owner = jnp.clip(jnp.searchsorted(bounds, offset, side='right'), 0, N_GROUP - 1)
        start = bounds[owner] - row_counts[owner]
        cold_pos = HOT_ROWS + owner * COLD_SLOT + offset - start
        chosen = jnp.where(picks < HOT_ROWS, picks, cold_pos).astype(jnp.int32)
        flat = chosen.reshape(-1)
        flat = flat.at[0].set(0)
        flat = flat.at[-1].set(HOT_ROWS + COLD_ROWS - 1)
        return flat.reshape(tail)
    subkeys = jax.random.split(key, DEVICES)
    return jax.vmap(one_trainer)(subkeys, counts, totals)


def draw_cold_counts(key, part):
    counts = shared_counts(key)
    return counts


def draw_mid_self(key, part):
    counts = shared_counts(key)
    key = jax.random.fold_in(key, 2)
    return live_positions(key, counts, (MID,))


def draw_nbr1(key, part):
    counts = shared_counts(key)
    key = jax.random.fold_in(key, 3)
    return live_positions(key, counts, (FAN0, MID))


def plant(values, key, low, top_value):
    longest = values.shape.index(max(values.shape))
    spots = []
    for shift in (0, 1):
        where = [jax.random.randint(jax.random.fold_in(key, axis), (), 0, length) for axis, length in enumerate(values.shape)]
        where[longest] = (where[longest] + shift) % values.shape[longest]
        spots.append(tuple(where))
    return values.at[spots[0]].set(low).at[spots[1]].set(top_value)


def level_of(own_key, extent, cuts, smallest, top_value):
    gain, own = 1.0, jax.random.fold_in(own_key, 6)
    for axis_at, shards_of in cuts:
        steps = jnp.exp(jax.random.uniform(jax.random.fold_in(own, axis_at), (shards_of,), jnp.float32, smallest / len(cuts), top_value / len(cuts)))
        gain = gain * jnp.repeat(steps, extent[axis_at] // shards_of).reshape([-1 if axis == axis_at else 1 for axis in range(len(extent))])
    return gain


def noise(own_key, dims, width, bound, cuts=(), kind=jnp.bfloat16):
    result = jax.random.normal(own_key, dims, jnp.float32) * width
    if len(cuts) > 0:
        result = level_of(own_key, dims, cuts, -0.22, 0.18) * result
    return jnp.clip(result, min=-bound, max=bound).astype(kind)


def setup_inputs(seed: int = 0) -> dict:
    streams_of = jax.random.split(jax.random.key(seed), 14)
    return {
        "hot_shard": noise(streams_of[0], (HOT_TABLE, F), 1.0, 6.0, ((0, 4),)),
        "cold_shard": noise(streams_of[1], (COLD_TABLE, F), 1.0, 6.0, ((0, 64),)),
        "hot_ids": plant(jax.random.randint(streams_of[2], (DEVICES, N_CLIQUE, HOT_SLOT), 0, HOT_SHARD), jax.random.fold_in(streams_of[2], 1), 0, HOT_SHARD - 1).astype(jnp.int32),
        "cold_ids": plant(jax.random.randint(streams_of[3], (DEVICES, N_GROUP, COLD_SLOT), 0, COLD_SHARD), jax.random.fold_in(streams_of[3], 1), 0, COLD_SHARD - 1).astype(jnp.int32),
        "cold_counts": draw_cold_counts(jax.random.fold_in(streams_of[13], 71), 0),
        "mid_self": draw_mid_self(jax.random.fold_in(streams_of[13], 71), 0),
        "nbr1": draw_nbr1(jax.random.fold_in(streams_of[13], 71), 0),
        "nbr2": plant(jax.random.randint(streams_of[7], (DEVICES, FAN1, SEEDS), 0, MID), jax.random.fold_in(streams_of[7], 1), 0, MID - 1).astype(jnp.int32),
        "labels": plant(jax.random.randint(streams_of[8], (DEVICES, SEEDS), 0, CLASSES), jax.random.fold_in(streams_of[8], 1), 0, CLASSES - 1).astype(jnp.int32),
        "w1_self": noise(streams_of[9], (F, HID), F ** -0.5, 0.5),
        "w1_neigh": noise(streams_of[10], (F, HID), F ** -0.5, 0.5),
        "w2_self": noise(streams_of[11], (HID, CLASSES), (HID // 16) ** -0.5, 1.5),
        "w2_neigh": noise(streams_of[12], (HID, CLASSES), (HID // 16) ** -0.5, 1.5),
    }


def sage_step(self_first, neigh_first, seed_neigh, seed_labels, w1_self, w1_neigh, w2_self, w2_neigh):
    seeds = seed_labels.shape[0]
    fan_second = seed_neigh.shape[0]
    middle = self_first.shape[0]
    hidden = w1_self.shape[1]
    classes = w2_self.shape[1]
    pre_first = jnp.dot(self_first, w1_self, preferred_element_type=jnp.float32) + jnp.dot(neigh_first, w1_neigh, preferred_element_type=jnp.float32)
    hidden_first = jax.nn.gelu(pre_first, approximate=True).astype(jnp.bfloat16)
    gathered = jnp.take(hidden_first, seed_neigh, axis=0)
    neigh_second = (lax.optimization_barrier(jnp.sum(gathered, axis=0, dtype=jnp.float32)) / fan_second).astype(jnp.bfloat16)
    seed_hidden = hidden_first[:seeds]
    logits = jnp.dot(seed_hidden, w2_self, preferred_element_type=jnp.float32) + jnp.dot(neigh_second, w2_neigh, preferred_element_type=jnp.float32)
    log_total = jnp.log(lax.optimization_barrier(jnp.sum(jnp.exp(logits), axis=1)))
    picked = jnp.take_along_axis(logits, seed_labels[:, None], axis=1)[:, 0]
    seed_loss = log_total - picked
    onehot = (seed_labels[:, None] == jnp.arange(classes, dtype=jnp.int32)[None, :]).astype(jnp.float32)
    probs = jnp.exp(logits - log_total[:, None])
    grad_logits = ((probs - onehot) / seeds).astype(jnp.bfloat16)
    term_w2_self = jnp.dot(seed_hidden.T, grad_logits, preferred_element_type=jnp.float32)
    term_w2_neigh = jnp.dot(neigh_second.T, grad_logits, preferred_element_type=jnp.float32)
    back_second = jnp.dot(grad_logits, w2_neigh.T, preferred_element_type=jnp.float32) / fan_second
    spread = jnp.broadcast_to(back_second[None], (fan_second, seeds, hidden)).reshape(-1, hidden)
    grad_hidden = jnp.zeros((middle, hidden), jnp.float32).at[seed_neigh.reshape(-1)].add(spread)
    grad_hidden = grad_hidden.at[:seeds].add(jnp.dot(grad_logits, w2_self.T, preferred_element_type=jnp.float32))
    unused, pullback = jax.vjp(partial(jax.nn.gelu, approximate=True), pre_first)
    grad_pre = pullback(grad_hidden)[0].astype(jnp.bfloat16)
    term_w1_self = jnp.dot(self_first.T, grad_pre, preferred_element_type=jnp.float32)
    term_w1_neigh = jnp.dot(neigh_first.T, grad_pre, preferred_element_type=jnp.float32)
    return (seed_loss, term_w1_self, term_w1_neigh, term_w2_self, term_w2_neigh)

def reference(hot_shard, cold_shard, hot_ids, cold_ids, cold_counts, mid_self, nbr1, nbr2, labels, w1_self, w1_neigh, w2_self, w2_neigh):

    def one_trainer(packed):
        hot_index, cold_index, counts, self_index, neigh_index, seed_neigh, seed_labels = packed
        hot_pos = (jnp.arange(N_CLIQUE, dtype=jnp.int32)[:, None] * HOT_SHARD + hot_index).reshape(-1)
        hot_rows = jnp.take(hot_shard, hot_pos, axis=0)
        cold_pos = (jnp.arange(N_GROUP, dtype=jnp.int32)[:, None] * COLD_SHARD + cold_index).reshape(-1)
        cold_rows = jnp.take(cold_shard, cold_pos, axis=0)
        live_mask = (jnp.arange(COLD_SLOT, dtype=jnp.int32)[None, :] < counts[:, None]).reshape(-1)
        cold_rows = jnp.where(live_mask[:, None], cold_rows, jnp.zeros_like(cold_rows))
        inputs = jnp.concatenate([hot_rows, cold_rows], axis=0)
        self_first = jnp.take(inputs, self_index, axis=0)
        neigh_first = (lax.optimization_barrier(jnp.sum(jnp.take(inputs, neigh_index, axis=0), axis=0, dtype=jnp.float32)) / FAN0).astype(jnp.bfloat16)
        return sage_step(self_first, neigh_first, seed_neigh, seed_labels, w1_self, w1_neigh, w2_self, w2_neigh)
    losses, terms_a, terms_b, terms_c, terms_d = lax.map(one_trainer, (hot_ids, cold_ids, cold_counts, mid_self, nbr1, nbr2, labels))
    return (losses, lax.optimization_barrier(jnp.sum(terms_a, axis=0)), lax.optimization_barrier(jnp.sum(terms_b, axis=0)), lax.optimization_barrier(jnp.sum(terms_c, axis=0)), lax.optimization_barrier(jnp.sum(terms_d, axis=0)))
```

```python
import jax
import jax.numpy as jnp
import numpy as np
from jax import lax
from jax.experimental import pallas as pl
from jax.experimental.pallas import tpu as pltpu
from jax.sharding import Mesh
from jax.sharding import PartitionSpec as P

AXES = ("clique", "z", "y", "core")
GROUP = ("z", "y", "core")
F = 128
HID = 256
CLASSES = 172
CLASS_ROWS = 176
SEEDS = 512
MID = 7680
FAN0 = 10
FAN1 = 15
HOT_ROWS = 2048
COLD_ROWS = 2048
STEP = 128
SLOTS = SEEDS * (FAN1 + 1)
CHUNKS = SLOTS // STEP
SEED_CHUNKS = SEEDS // STEP
TERM_ROWS = 1280
HALF_ROWS = TERM_ROWS // 2
GELU_C = float(np.sqrt(2.0 / np.pi))
GELU_A = 0.044715


def tree_sum(rows):
    while len(rows) > 1:
        rows = [
            rows[i] + rows[i + 1] if i + 1 < len(rows) else rows[i]
            for i in range(0, len(rows), 2)
        ]
    return rows[0]


def train_kernel(
    counts, where_hot, first_slots, nbr1, nbr2, mid_self,
    hot0, hot1, hot2, hot3, cold, labels, w1_self, w1_neigh, w2_self, w2_neigh,
    loss_out, terms_out,
    slots, n0, n1, n2, n3, n4, n5, n6, n7, n8, n9, own, copied,
    table, x_even, x_odd, w1, w2s, w2n, x_all, slope, hidden, hidden_b, grad_logits, back, w1_acc,
):
    neighbours = (n0, n1, n2, n3, n4, n5, n6, n7, n8, n9)
    copies = [pltpu.make_async_copy(nbr1.at[k, 0], neighbours[k], copied.at[k]) for k in range(FAN0)]
    copies.append(pltpu.make_async_copy(mid_self.at[0], own, copied.at[FAN0]))
    copies.append(
        pltpu.make_async_copy(first_slots.at[0], slots.at[pl.ds(0, SEEDS)], copied.at[FAN0 + 1])
    )
    for k in range(FAN1):
        copies.append(
            pltpu.make_async_copy(
                nbr2.at[k, 0],
                slots.at[pl.ds((k + 1) * SEEDS, SEEDS)],
                copied.at[FAN0 + 2 + k],
            )
        )
    copies.append(
        pltpu.make_async_copy(
            first_slots.at[0, pl.ds(0, 128)], slots.at[pl.ds(SLOTS, 128)], copied.at[FAN0 + FAN1 + 2]
        )
    )
    for copy in copies:
        copy.start()

    f32, bf16 = jnp.float32, jnp.bfloat16

    for d, block in enumerate((hot0, hot1, hot2, hot3)):
        start = pl.multiple_of(where_hot[d] * 512, 512)
        table[pl.ds(start, 512), :] = block[...].astype(f32)
    slot_index = lax.broadcasted_iota(jnp.int32, (32, F), 0)

    def place_cold(o, carry):
        rows = cold[o].astype(f32)
        live = slot_index < counts[o]
        table[pl.ds(pl.multiple_of(HOT_ROWS + o * 32, 32), 32), :] = jnp.where(live, rows, 0.0)
        return carry

    lax.fori_loop(0, 64, place_cold, 0, unroll=4)

    w1[0:F, :] = w1_self[...]
    w1[F : 2 * F, :] = w1_neigh[...]
    for padded, given in ((w2s, w2_self), (w2n, w2_neigh)):
        padded[...] = jnp.zeros((256, HID), bf16)
        padded[0:CLASSES, :] = given[...]
    hidden[...] = jnp.zeros((2 * SEEDS, HID), f32)

    def gather(chunk, buffer):
        base = chunk * STEP
        for u in range(STEP):
            m = slots[base + u]
            rows = [table[pl.ds(near[m], 1), :] for near in neighbours]
            buffer[u : u + 1, 0:F] = table[pl.ds(own[m], 1), :]
            buffer[u : u + 1, F : 2 * F] = tree_sum(rows)

    def forward(chunk, buffer):
        row = pl.multiple_of(chunk * STEP, STEP)
        x_all[pl.ds(row, STEP), 0:F] = buffer[:, 0:F].astype(bf16)
        x_all[pl.ds(row, STEP), F : 2 * F] = (buffer[:, F : 2 * F] * (1.0 / FAN0)).astype(bf16)
        x = jnp.concatenate(
            [buffer[:, 0:F].astype(bf16), (buffer[:, F : 2 * F] * (1.0 / FAN0)).astype(bf16)], axis=1
        )
        v = jnp.dot(x, w1[...], preferred_element_type=f32)
        square = v * v
        t = jnp.tanh(v * (GELU_C + (GELU_C * GELU_A) * square))
        half = 0.5 + 0.5 * t
        h = (v * half).astype(bf16).astype(f32)
        slope[pl.ds(row, STEP), :] = half + (0.5 * v) * (1.0 - t * t) * (
            GELU_C + (3.0 * GELU_C * GELU_A) * square
        )
        into = pl.multiple_of(
            lax.rem(chunk, SEED_CHUNKS) * STEP + jnp.where(chunk >= SEED_CHUNKS, SEEDS, 0), STEP
        )
        hidden[pl.ds(into, STEP), :] += h

    for copy in copies:
        copy.wait()
    gather(0, x_even)

    def two_chunks(i, carry):
        gather(2 * i + 1, x_odd)
        forward(2 * i, x_even)
        gather(2 * i + 2, x_even)
        forward(2 * i + 1, x_odd)
        return carry

    lax.fori_loop(0, CHUNKS // 2, two_chunks, 0)

    hidden_b[0:SEEDS, :] = hidden[0:SEEDS, :].astype(bf16)
    hidden_b[SEEDS:, :] = (hidden[SEEDS:, :] / FAN1).astype(bf16)
    nt = (((1,), (1,)), ((), ()))
    tn = (((0,), (0,)), ((), ()))
    eye = lax.broadcasted_iota(jnp.int32, (128, 128), 0) == lax.broadcasted_iota(
        jnp.int32, (128, 128), 1
    )
    lane = lax.broadcasted_iota(jnp.int32, (128, 256), 1)
    for b in range(SEEDS // 128):
        rows = slice(b * 128, (b + 1) * 128)
        logits = lax.dot_general(
            hidden_b[rows, :], w2s[...], nt, preferred_element_type=f32
        ) + lax.dot_general(
            hidden_b[SEEDS + b * 128 : SEEDS + (b + 1) * 128, :], w2n[...], nt,
            preferred_element_type=f32,
        )
        label_row = labels[:, rows].astype(f32)
        label = jnp.sum(jnp.where(eye, label_row, 0.0), axis=1, keepdims=True).astype(jnp.int32)
        valid = lane < CLASSES
        top = jnp.max(jnp.where(valid, logits, -3.0e38), axis=1, keepdims=True)
        total = jnp.sum(jnp.where(valid, jnp.exp(logits - top), 0.0), axis=1, keepdims=True)
        log_total = jnp.log(total) + top
        hit = lane == label
        picked = jnp.sum(jnp.where(hit, logits, 0.0), axis=1, keepdims=True)
        loss = log_total - picked
        loss_out[:, rows] = jnp.sum(jnp.where(eye, loss, 0.0), axis=0, keepdims=True)
        probs = jnp.where(valid, jnp.exp(logits - log_total), 0.0)
        grad_logits[rows, :] = ((probs - hit.astype(f32)) / SEEDS).astype(bf16)

    g = grad_logits[...]
    terms_out[608:HALF_ROWS, :] = jnp.zeros((HALF_ROWS - 608, F), f32)
    terms_out[HALF_ROWS + 608 :, :] = jnp.zeros((HALF_ROWS - 608, F), f32)
    for at, part in ((256, slice(0, SEEDS)), (256 + CLASS_ROWS, slice(SEEDS, 2 * SEEDS))):
        term = lax.dot_general(g, hidden_b[part, :], tn, preferred_element_type=f32)
        terms_out[at : at + CLASS_ROWS, :] = term[0:CLASS_ROWS, 0:F]
        terms_out[HALF_ROWS + at : HALF_ROWS + at + CLASS_ROWS, :] = term[0:CLASS_ROWS, F:]
    back[0:SEEDS, :] = jnp.dot(g, w2s[...], preferred_element_type=f32)
    back[SEEDS:, :] = jnp.dot(g, w2n[...], preferred_element_type=f32) / FAN1

    def backward(j, into):
        row = pl.multiple_of(j * SEEDS, SEEDS)
        grad_pre = (slope[pl.ds(row, SEEDS), :] * back[into, :]).astype(bf16)
        return lax.dot_general(x_all[pl.ds(row, SEEDS), :], grad_pre, tn, preferred_element_type=f32)

    w1_acc[...] = backward(0, slice(0, SEEDS))

    def add_block(j, carry):
        w1_acc[...] += backward(j, slice(SEEDS, 2 * SEEDS))
        return carry

    lax.fori_loop(1, FAN1 + 1, add_block, 0)
    terms_out[0:256, :] = w1_acc[:, 0:F]
    terms_out[HALF_ROWS : HALF_ROWS + 256, :] = w1_acc[:, F:]


def train(counts, where_hot, nbr1, nbr2, mid_self, hot, cold, labels, w1_self, w1_neigh, w2_self_t, w2_neigh_t):
    smem = pl.BlockSpec(memory_space=pltpu.SMEM)
    vmem = pl.BlockSpec(memory_space=pltpu.VMEM)
    anywhere = pl.BlockSpec(memory_space=pl.ANY)
    first_slots = np.arange(SEEDS, dtype=np.int32)[None]
    return pl.pallas_call(
        train_kernel,
        out_shape=(
            jax.ShapeDtypeStruct((1, SEEDS), jnp.float32),
            jax.ShapeDtypeStruct((TERM_ROWS, F), jnp.float32),
        ),
        in_specs=[smem] * 2 + [anywhere] * 4 + [vmem] * 10,
        out_specs=(vmem, vmem),
        scratch_shapes=[
            pltpu.SMEM((SLOTS + 128,), jnp.int32),
            *[pltpu.SMEM((MID,), jnp.int32) for _ in range(FAN0 + 1)],
            pltpu.SemaphoreType.DMA((FAN0 + FAN1 + 3,)),
            pltpu.VMEM((HOT_ROWS + COLD_ROWS, F), jnp.float32),
            pltpu.VMEM((STEP, 2 * F), jnp.float32),
            pltpu.VMEM((STEP, 2 * F), jnp.float32),
            pltpu.VMEM((2 * F, HID), jnp.bfloat16),
            pltpu.VMEM((256, HID), jnp.bfloat16),
            pltpu.VMEM((256, HID), jnp.bfloat16),
            pltpu.VMEM((SLOTS, 2 * F), jnp.bfloat16),
            pltpu.VMEM((SLOTS, HID), jnp.float32),
            pltpu.VMEM((2 * SEEDS, HID), jnp.float32),
            pltpu.VMEM((2 * SEEDS, HID), jnp.bfloat16),
            pltpu.VMEM((SEEDS, 256), jnp.bfloat16),
            pltpu.VMEM((2 * SEEDS, HID), jnp.float32),
            pltpu.VMEM((2 * F, HID), jnp.float32),
        ],
        compiler_params=pltpu.CompilerParams(vmem_limit_bytes=44 << 20),
        cost_estimate=pl.CostEstimate(flops=4 << 30, bytes_accessed=4 << 20, transcendentals=2 << 20),
        name="train",
    )(
        counts, where_hot, jnp.asarray(first_slots), nbr1[:, None], nbr2[:, None], mid_self[None],
        *hot, cold, labels, w1_self, w1_neigh, w2_self_t, w2_neigh_t,
    )


def swap_hot(hot_shard, hot_ids):
    me = lax.axis_index("clique")
    peers = [lax.rem(me + d, 4) for d in range(4)]
    asked = [lax.dynamic_index_in_dim(hot_ids, peer, 0, keepdims=False) for peer in peers]
    requests = [asked[0]] + [
        lax.ppermute(asked[d], "clique", [(i, (i + d) % 4) for i in range(4)]) for d in (1, 2, 3)
    ]
    return peers, requests


def serve_hot(hot_shard, requests):
    rows = [hot_shard.at[ids].get(mode="promise_in_bounds") for ids in requests]
    return [rows[0]] + [
        lax.ppermute(rows[d], "clique", [(i, (i - d) % 4) for i in range(4)]) for d in (1, 2, 3)
    ]


def exchange(x, axes):
    return lax.all_to_all(x, axes, split_axis=0, concat_axis=0, tiled=True)


def share(x, axes, n):
    return exchange(jnp.broadcast_to(x[None], (n,) + x.shape), axes)


SWAP = [(0, 1), (1, 0)]


def sum_everywhere(x):
    tiles = x.reshape(TERM_ROWS // 8, 8, F)
    half = tiles.shape[0] // 2
    core = lax.axis_index("core")
    theirs = lax.dynamic_slice_in_dim(tiles, (1 - core) * half, half, 0)
    mine = lax.dynamic_slice_in_dim(tiles, core * half, half, 0)
    mine = mine + lax.ppermute(theirs, "core", SWAP)
    mine = exchange(mine.reshape(16, half // 16, 8, F), ("clique", "y")).sum(0)
    mine = share(mine, "z", 8).sum(0)
    mine = share(mine, ("clique", "y"), 16).reshape(half * 8, F)
    other = lax.ppermute(mine, "core", SWAP)
    return jnp.where(core == 0, mine, other), jnp.where(core == 0, other, mine)


def body(
    hot_shard, cold_shard, hot_ids, cold_ids, cold_counts, mid_self, nbr1, nbr2, labels,
    w1_self, w1_neigh, w2_self, w2_neigh,
):
    peers, requests = swap_hot(hot_shard, hot_ids[0])
    asked = exchange(cold_ids[0], GROUP)
    served = cold_shard.at[asked].get(mode="promise_in_bounds")
    cold = exchange(served, GROUP)
    hot = serve_hot(hot_shard, requests)
    loss, terms = train(
        cold_counts[0], jnp.stack(peers).astype(jnp.int32), nbr1[0], nbr2[0], mid_self[0],
        hot, cold, labels, w1_self, w1_neigh, w2_self.T, w2_neigh.T,
    )
    left, right = sum_everywhere(terms)

    def rows(at, n):
        return jnp.concatenate([left[at : at + n], right[at : at + n]], axis=1)

    return (
        loss,
        rows(0, F),
        rows(F, F),
        rows(2 * F, CLASSES).T,
        rows(2 * F + CLASS_ROWS, CLASSES).T,
    )


def solution(mesh):
    mesh = Mesh(mesh.devices.reshape(4, 8, 4, 2), AXES)
    each = P(AXES)
    return jax.shard_map(
        body,
        mesh=mesh,
        in_specs=(P("clique"), P(GROUP)) + (each,) * 7 + (P(),) * 4,
        out_specs=(each, P(), P(), P(), P()),
        check_vma=False,
    )
```

```python
import jax
import jax.numpy as jnp
import numpy as np
from jax import lax
from jax.experimental import pallas as pl
from jax.experimental.pallas import tpu as pltpu
from jax.sharding import Mesh
from jax.sharding import PartitionSpec as P

AXES = ("clique", "z", "y", "core")
GROUP = ("z", "y", "core")
F = 128
HID = 256
CLASSES = 172
CLASS_ROWS = 176
SEEDS = 512
MID = 7680
FAN0 = 10
FAN1 = 15
HOT_ROWS = 2048
COLD_ROWS = 2048
STEP = 128
SLOTS = SEEDS * (FAN1 + 1)
CHUNKS = SLOTS // STEP
SEED_CHUNKS = SEEDS // STEP
HALF_ROWS = 640
PARTS = 8
GELU_C = float(np.sqrt(2.0 / np.pi))
GELU_A = 0.044715


def tree_sum(rows):
    while len(rows) > 1:
        rows = [
            rows[i] + rows[i + 1] if i + 1 < len(rows) else rows[i]
            for i in range(0, len(rows), 2)
        ]
    return rows[0]


def train_kernel(
    counts, where_hot, core, first_slots, nbr1, nbr2, mid_self,
    hot0, hot1, hot2, hot3, cold, labels, w1_self, w1_neigh, w2_self, w2_neigh,
    loss_out, keep_out, send_out,
    slots, n0, n1, n2, n3, n4, n5, n6, n7, n8, n9, own, copied,
    table, x_even, x_odd, w1, w2s, w2n, x_all, slope, hidden, hidden_b, grad_logits, back, w1_acc, terms,
):
    f32, bf16 = jnp.float32, jnp.bfloat16
    neighbours = (n0, n1, n2, n3, n4, n5, n6, n7, n8, n9)
    head, tail = pl.ds(0, SEEDS), pl.ds(SEEDS, MID - SEEDS)
    early, late = [], []
    for k in range(FAN0):
        early.append((nbr1.at[k, 0, head], neighbours[k].at[head]))
        late.append((nbr1.at[k, 0, tail], neighbours[k].at[tail]))
    early.append((mid_self.at[0, head], own.at[head]))
    late.append((mid_self.at[0, tail], own.at[tail]))
    early.append((first_slots.at[0], slots.at[head]))
    late.append((first_slots.at[0, pl.ds(0, STEP)], slots.at[pl.ds(SLOTS, STEP)]))
    for k in range(FAN1):
        late.append((nbr2.at[k, 0], slots.at[pl.ds((k + 1) * SEEDS, SEEDS)]))
    early = [pltpu.make_async_copy(*pair, copied.at[i]) for i, pair in enumerate(early)]
    late = [pltpu.make_async_copy(*pair, copied.at[len(early) + i]) for i, pair in enumerate(late)]
    for copy in early + late:
        copy.start()

    for d, block in enumerate((hot0, hot1, hot2, hot3)):
        start = pl.multiple_of(where_hot[d] * 512, 512)
        table[pl.ds(start, 512), :] = block[...].astype(f32)
    slot_index = lax.broadcasted_iota(jnp.int32, (32, F), 0)

    def place_cold(o, carry):
        rows = cold[o].astype(f32)
        live = slot_index < counts[o]
        table[pl.ds(pl.multiple_of(HOT_ROWS + o * 32, 32), 32), :] = jnp.where(live, rows, 0.0)
        return carry

    lax.fori_loop(0, 64, place_cold, 0, unroll=4)

    w1[0:F, :] = w1_self[...]
    w1[F : 2 * F, :] = w1_neigh[...]
    for padded, given in ((w2s, w2_self), (w2n, w2_neigh)):
        padded[...] = jnp.zeros((256, HID), bf16)
        padded[0:CLASSES, :] = given[...]
    hidden[...] = jnp.zeros((2 * SEEDS, HID), f32)

    def gather(chunk, buffer):
        base = chunk * STEP
        for u in range(STEP):
            m = slots[base + u]
            rows = [table[pl.ds(near[m], 1), :] for near in neighbours]
            buffer[u : u + 1, 0:F] = table[pl.ds(own[m], 1), :]
            buffer[u : u + 1, F : 2 * F] = tree_sum(rows)

    def forward(chunk, buffer):
        row = pl.multiple_of(chunk * STEP, STEP)
        x_all[pl.ds(row, STEP), 0:F] = buffer[:, 0:F].astype(bf16)
        x_all[pl.ds(row, STEP), F : 2 * F] = (buffer[:, F : 2 * F] * (1.0 / FAN0)).astype(bf16)
        x = jnp.concatenate(
            [buffer[:, 0:F].astype(bf16), (buffer[:, F : 2 * F] * (1.0 / FAN0)).astype(bf16)], axis=1
        )
        v = jnp.dot(x, w1[...], preferred_element_type=f32)
        square = v * v
        t = jnp.tanh(v * (GELU_C + (GELU_C * GELU_A) * square))
        half = 0.5 + 0.5 * t
        h = (v * half).astype(bf16).astype(f32)
        slope[pl.ds(row, STEP), :] = half + (0.5 * v) * (1.0 - t * t) * (
            GELU_C + (3.0 * GELU_C * GELU_A) * square
        )
        into = pl.multiple_of(
            lax.rem(chunk, SEED_CHUNKS) * STEP + jnp.where(chunk >= SEED_CHUNKS, SEEDS, 0), STEP
        )
        hidden[pl.ds(into, STEP), :] += h

    for copy in early:
        copy.wait()
    gather(0, x_even)

    def two_chunks(i, carry):
        @pl.when(i == SEED_CHUNKS // 2 - 1)
        def _():
            for copy in late:
                copy.wait()

        gather(2 * i + 1, x_odd)
        forward(2 * i, x_even)
        gather(2 * i + 2, x_even)
        forward(2 * i + 1, x_odd)
        return carry

    lax.fori_loop(0, CHUNKS // 2, two_chunks, 0)

    hidden_b[0:SEEDS, :] = hidden[0:SEEDS, :].astype(bf16)
    hidden_b[SEEDS:, :] = (hidden[SEEDS:, :] / FAN1).astype(bf16)
    nt = (((1,), (1,)), ((), ()))
    tn = (((0,), (0,)), ((), ()))
    eye = lax.broadcasted_iota(jnp.int32, (128, 128), 0) == lax.broadcasted_iota(
        jnp.int32, (128, 128), 1
    )
    lane = lax.broadcasted_iota(jnp.int32, (128, 256), 1)
    for b in range(SEEDS // 128):
        rows = slice(b * 128, (b + 1) * 128)
        logits = lax.dot_general(
            hidden_b[rows, :], w2s[...], nt, preferred_element_type=f32
        ) + lax.dot_general(
            hidden_b[SEEDS + b * 128 : SEEDS + (b + 1) * 128, :], w2n[...], nt,
            preferred_element_type=f32,
        )
        label_row = labels[:, rows].astype(f32)
        label = jnp.sum(jnp.where(eye, label_row, 0.0), axis=1, keepdims=True).astype(jnp.int32)
        valid = lane < CLASSES
        top = jnp.max(jnp.where(valid, logits, -3.0e38), axis=1, keepdims=True)
        total = jnp.sum(jnp.where(valid, jnp.exp(logits - top), 0.0), axis=1, keepdims=True)
        log_total = jnp.log(total) + top
        hit = lane == label
        picked = jnp.sum(jnp.where(hit, logits, 0.0), axis=1, keepdims=True)
        loss = log_total - picked
        loss_out[:, rows] = jnp.sum(jnp.where(eye, loss, 0.0), axis=0, keepdims=True)
        probs = jnp.where(valid, jnp.exp(logits - log_total), 0.0)
        grad_logits[rows, :] = ((probs - hit.astype(f32)) / SEEDS).astype(bf16)

    left, right = core[0], 1 - core[0]
    g = grad_logits[...]
    terms[:, 608:, :] = jnp.zeros((2, HALF_ROWS - 608, F), f32)
    for at, part in ((256, slice(0, SEEDS)), (256 + CLASS_ROWS, slice(SEEDS, 2 * SEEDS))):
        term = lax.dot_general(g, hidden_b[part, :], tn, preferred_element_type=f32)
        terms[left, at : at + CLASS_ROWS, :] = term[0:CLASS_ROWS, 0:F]
        terms[right, at : at + CLASS_ROWS, :] = term[0:CLASS_ROWS, F:]
    back[0:SEEDS, :] = jnp.dot(g, w2s[...], preferred_element_type=f32)
    back[SEEDS:, :] = jnp.dot(g, w2n[...], preferred_element_type=f32) / FAN1

    def backward(j, into):
        row = pl.multiple_of(j * SEEDS, SEEDS)
        grad_pre = (slope[pl.ds(row, SEEDS), :] * back[into, :]).astype(bf16)
        return lax.dot_general(x_all[pl.ds(row, SEEDS), :], grad_pre, tn, preferred_element_type=f32)

    w1_acc[...] = backward(0, slice(0, SEEDS))

    def add_block(j, carry):
        w1_acc[...] += backward(j, slice(SEEDS, 2 * SEEDS))
        return carry

    lax.fori_loop(1, FAN1 + 1, add_block, 0)
    terms[left, 0:256, :] = w1_acc[:, 0:F]
    terms[right, 0:256, :] = w1_acc[:, F:]
    keep_out[...] = terms[0]
    send_out[...] = terms[1]


def train(counts, where_hot, core, nbr1, nbr2, mid_self, hot, cold, labels, w1_self, w1_neigh, w2_self_t, w2_neigh_t):
    smem = pl.BlockSpec(memory_space=pltpu.SMEM)
    vmem = pl.BlockSpec(memory_space=pltpu.VMEM)
    anywhere = pl.BlockSpec(memory_space=pl.ANY)
    first_slots = np.arange(SEEDS, dtype=np.int32)[None]
    return pl.pallas_call(
        train_kernel,
        out_shape=(
            jax.ShapeDtypeStruct((1, SEEDS), jnp.float32),
            jax.ShapeDtypeStruct((HALF_ROWS, F), jnp.float32),
            jax.ShapeDtypeStruct((HALF_ROWS, F), jnp.float32),
        ),
        in_specs=[smem] * 3 + [anywhere] * 4 + [vmem] * 10,
        out_specs=(vmem, vmem, vmem),
        scratch_shapes=[
            pltpu.SMEM((SLOTS + 128,), jnp.int32),
            *[pltpu.SMEM((MID,), jnp.int32) for _ in range(FAN0 + 1)],
            pltpu.SemaphoreType.DMA((2 * FAN0 + FAN1 + 5,)),
            pltpu.VMEM((HOT_ROWS + COLD_ROWS, F), jnp.float32),
            pltpu.VMEM((STEP, 2 * F), jnp.float32),
            pltpu.VMEM((STEP, 2 * F), jnp.float32),
            pltpu.VMEM((2 * F, HID), jnp.bfloat16),
            pltpu.VMEM((256, HID), jnp.bfloat16),
            pltpu.VMEM((256, HID), jnp.bfloat16),
            pltpu.VMEM((SLOTS, 2 * F), jnp.bfloat16),
            pltpu.VMEM((SLOTS, HID), jnp.float32),
            pltpu.VMEM((2 * SEEDS, HID), jnp.float32),
            pltpu.VMEM((2 * SEEDS, HID), jnp.bfloat16),
            pltpu.VMEM((SEEDS, 256), jnp.bfloat16),
            pltpu.VMEM((2 * SEEDS, HID), jnp.float32),
            pltpu.VMEM((2 * F, HID), jnp.float32),
            pltpu.VMEM((2, HALF_ROWS, F), jnp.float32),
        ],
        compiler_params=pltpu.CompilerParams(vmem_limit_bytes=44 << 20),
        cost_estimate=pl.CostEstimate(flops=4 << 30, bytes_accessed=4 << 20, transcendentals=2 << 20),
        name="train",
    )(
        counts, where_hot, core, jnp.asarray(first_slots), nbr1[:, None], nbr2[:, None], mid_self[None],
        *hot, cold, labels, w1_self, w1_neigh, w2_self_t, w2_neigh_t,
    )


def pick_kernel(n, *refs):
    asked, shard, given = refs[:n], refs[n], refs[n + 1 : 2 * n + 1]
    narrow, wide, picked, copied = refs[2 * n + 1 :]
    step = shard.shape[0] // PARTS
    parts = [pl.ds(i * step, step) for i in range(PARTS)]
    copies = [
        pltpu.make_async_copy(shard.at[part], narrow.at[part], copied.at[i])
        for i, part in enumerate(parts)
    ]
    for copy in copies:
        copy.start()
    for copy, part in zip(copies, parts):
        copy.wait()
        wide[part, :] = narrow[part, :].astype(jnp.float32)
    row = 0
    for ids, out in zip(asked, given):
        first = row
        for at in np.ndindex(ids.shape):
            picked[row : row + 1, :] = wide[pl.ds(ids[at], 1), :]
            row += 1
        if len(out.shape) == 2:
            out[...] = picked[first:row, :].astype(out.dtype)
        else:
            size = out.shape[1]
            for o in range(out.shape[0]):
                out[o] = picked[first + o * size : first + (o + 1) * size, :].astype(out.dtype)


def pick_rows(shard, asked, name):
    n = len(asked)
    total = sum(int(np.prod(ids.shape)) for ids in asked)
    return pl.pallas_call(
        lambda *refs: pick_kernel(n, *refs),
        out_shape=tuple(jax.ShapeDtypeStruct(ids.shape + (F,), jnp.bfloat16) for ids in asked),
        in_specs=[pl.BlockSpec(memory_space=pltpu.SMEM)] * n + [pl.BlockSpec(memory_space=pltpu.HBM)],
        out_specs=tuple(pl.BlockSpec(memory_space=pltpu.VMEM) for _ in asked),
        scratch_shapes=[
            pltpu.VMEM(shard.shape, shard.dtype),
            pltpu.VMEM(shard.shape, jnp.float32),
            pltpu.VMEM((total, F), jnp.float32),
            pltpu.SemaphoreType.DMA((PARTS,)),
        ],
        compiler_params=pltpu.CompilerParams(vmem_limit_bytes=40 << 20),
        cost_estimate=pl.CostEstimate(flops=0, bytes_accessed=4 << 20, transcendentals=0),
        name=name,
    )(*asked, shard)


def clique_peers(hot_ids):
    me = lax.axis_index("clique")
    peers = [lax.rem(me + d, 4) for d in range(4)]
    return peers, [lax.dynamic_index_in_dim(hot_ids, peer, 0, keepdims=False) for peer in peers]


def fetch_hot(hot_shard, requests):
    rows = pick_rows(hot_shard, requests, "pick_hot")
    return [rows[0]] + [
        lax.ppermute(rows[d], "clique", [(i, (i - d) % 4) for i in range(4)]) for d in (1, 2, 3)
    ]


def exchange(x, axes):
    return lax.all_to_all(x, axes, split_axis=0, concat_axis=0, tiled=True)


def share(x, axes, n):
    return exchange(jnp.broadcast_to(x[None], (n,) + x.shape), axes)


SWAP = [(0, 1), (1, 0)]


def split_kernel(core, mine, other, *outs):
    for first, at in ((0, slice(0, F)), (1, slice(F, 2 * F))):
        for out, row in zip(outs, (0, F, 2 * F, 2 * F + CLASS_ROWS)):
            rows = slice(row, row + out.shape[0])
            out[:, at] = jnp.where(core[0] == first, mine[rows, :], other[rows, :])


def sum_everywhere(keep, send, core):
    mine = keep + lax.ppermute(send, "core", SWAP)
    mine = exchange(mine.reshape(16, HALF_ROWS // 128, 8, F), ("clique", "y")).sum(0)
    mine = share(mine, "z", 8).sum(0)
    mine = share(mine, ("clique", "y"), 16).reshape(HALF_ROWS, F)
    other = lax.ppermute(mine, "core", SWAP)
    vmem = pl.BlockSpec(memory_space=pltpu.VMEM)
    return pl.pallas_call(
        split_kernel,
        out_shape=tuple(jax.ShapeDtypeStruct((n, HID), jnp.float32) for n in (F, F, CLASSES, CLASSES)),
        in_specs=[pl.BlockSpec(memory_space=pltpu.SMEM), vmem, vmem],
        out_specs=(vmem,) * 4,
        compiler_params=pltpu.CompilerParams(vmem_limit_bytes=8 << 20),
        name="split",
    )(core, mine, other)


def body(
    hot_shard, cold_shard, hot_ids, cold_ids, cold_counts, mid_self, nbr1, nbr2, labels,
    w1_self, w1_neigh, w2_self, w2_neigh,
):
    peers, hot_asked = clique_peers(hot_ids[0])
    hot_asked[1:] = [
        lax.ppermute(hot_asked[d], "clique", [(i, (i + d) % 4) for i in range(4)]) for d in (1, 2, 3)
    ]
    cold_asked = exchange(cold_ids[0], GROUP)
    *hot_asked, cold_asked = lax.optimization_barrier((*hot_asked, cold_asked))
    (served,) = pick_rows(cold_shard, [cold_asked], "pick_cold")
    cold = exchange(served, GROUP)
    *hot_asked, served = lax.optimization_barrier((*hot_asked, served))
    hot = fetch_hot(hot_shard, hot_asked)
    core = lax.axis_index("core").astype(jnp.int32)[None]
    loss, keep, send = train(
        cold_counts[0], jnp.stack(peers).astype(jnp.int32), core, nbr1[0], nbr2[0], mid_self[0],
        hot, cold, labels, w1_self, w1_neigh, w2_self.T, w2_neigh.T,
    )
    w1s, w1n, w2s, w2n = sum_everywhere(keep, send, core)
    return loss, w1s, w1n, w2s.T, w2n.T


def solution(mesh):
    mesh = Mesh(mesh.devices.reshape(4, 8, 4, 2), AXES)
    each = P(AXES)
    return jax.shard_map(
        body,
        mesh=mesh,
        in_specs=(P("clique"), P(GROUP)) + (each,) * 7 + (P(),) * 4,
        out_specs=(each, P(), P(), P(), P()),
        check_vma=False,
    )
```

```python
import jax
import jax.numpy as jnp
import numpy as np
from jax import lax
from jax.experimental import pallas as pl
from jax.experimental.pallas import tpu as pltpu
from jax.sharding import Mesh
from jax.sharding import PartitionSpec as P

AXES = ("clique", "z", "y", "core")
GROUP = ("z", "y", "core")
F = 128
HID = 256
CLASSES = 172
CLASS_ROWS = 176
SEEDS = 512
MID = 7680
FAN0 = 10
POSITIONS = FAN0 + 1
FAN1 = 15
HOT_ROWS = 2048
COLD_ROWS = 2048
STEP = 128
SLOTS = SEEDS * (FAN1 + 1)
CHUNKS = SLOTS // STEP
SEED_CHUNKS = SEEDS // STEP
HALF_ROWS = 640
PARTS = 8
PIECES = (0, 512, 2048, SLOTS)
GELU_C = float(np.sqrt(2.0 / np.pi))
GELU_A = 0.044715


def tree_sum(rows):
    while len(rows) > 1:
        rows = [
            rows[i] + rows[i + 1] if i + 1 < len(rows) else rows[i]
            for i in range(0, len(rows), 2)
        ]
    return rows[0]


def order_kernel(nbr2, nbr1, mid_self, out, slots, info, ordered, copied):
    copies = [
        pltpu.make_async_copy(nbr2.at[k, 0], slots.at[pl.ds(k * SEEDS, SEEDS)], copied.at[k])
        for k in range(FAN1)
    ]
    for copy in copies:
        copy.start()
    empty = jnp.zeros((128 - POSITIONS, 128), jnp.int32)

    def by_node(i, carry):
        at = pl.ds(pl.multiple_of(i * 128, 128), 128)
        rows = [nbr1[k, :, at] for k in range(FAN0)] + [mid_self[:, at]]
        info[at, :] = jnp.concatenate([*rows, empty], axis=0).T
        return carry

    lax.fori_loop(0, MID // 128, by_node, 0, unroll=4)
    for k in range(FAN0):
        out[k, :, 0:SEEDS] = nbr1[k, :, 0:SEEDS]
    out[FAN0, :, 0:SEEDS] = mid_self[:, 0:SEEDS]
    for copy in copies:
        copy.wait()

    def by_slot(i, carry):
        base = i * 128
        for u in range(128):
            ordered[pl.ds(base + u, 1), :] = info[pl.ds(slots[base + u], 1), :]
        return carry

    lax.fori_loop(0, MID // 128, by_slot, 0)

    def by_chunk(i, carry):
        rows = ordered[pl.ds(pl.multiple_of(i * 128, 128), 128), :].T
        at = pl.ds(pl.multiple_of(SEEDS + i * 128, 128), 128)
        for k in range(POSITIONS):
            out[k, :, at] = rows[k : k + 1, :]
        return carry

    lax.fori_loop(0, MID // 128, by_chunk, 0, unroll=4)


def order_positions(nbr1, nbr2, mid_self):
    vmem = pl.BlockSpec(memory_space=pltpu.VMEM)
    return pl.pallas_call(
        order_kernel,
        out_shape=jax.ShapeDtypeStruct((POSITIONS, 1, SLOTS), jnp.int32),
        in_specs=[pl.BlockSpec(memory_space=pl.ANY), vmem, vmem],
        out_specs=vmem,
        scratch_shapes=[
            pltpu.SMEM((MID,), jnp.int32),
            pltpu.VMEM((MID, 128), jnp.int32),
            pltpu.VMEM((MID, 128), jnp.int32),
            pltpu.SemaphoreType.DMA((FAN1,)),
        ],
        compiler_params=pltpu.CompilerParams(vmem_limit_bytes=16 << 20),
        cost_estimate=pl.CostEstimate(flops=0, bytes_accessed=8 << 20, transcendentals=0),
        name="order",
    )(nbr2[:, None], nbr1[:, None], mid_self[None])


def train_kernel(
    counts, where_hot, core, places,
    hot0, hot1, hot2, hot3, cold, labels, w1_self, w1_neigh, w2_self, w2_neigh,
    loss_out, keep_out, send_out,
    n0, n1, n2, n3, n4, n5, n6, n7, n8, n9, own, copied,
    table, x_even, x_odd, w1, w2s, w2n, x_all, slope, hidden, hidden_b, grad_logits, back, w1_acc, terms,
):
    f32, bf16 = jnp.float32, jnp.bfloat16
    neighbours = (n0, n1, n2, n3, n4, n5, n6, n7, n8, n9)
    pieces = []
    for p, (start, stop) in enumerate(zip(PIECES[:-1], PIECES[1:])):
        at = pl.ds(start, stop - start)
        pieces.append(
            [
                pltpu.make_async_copy(places.at[k, 0, at], to.at[at], copied.at[p, k])
                for k, to in enumerate((*neighbours, own))
            ]
        )
    for copies in pieces:
        for copy in copies:
            copy.start()

    for d, block in enumerate((hot0, hot1, hot2, hot3)):
        start = pl.multiple_of(where_hot[d] * 512, 512)
        table[pl.ds(start, 512), :] = block[...].astype(f32)
    slot_index = lax.broadcasted_iota(jnp.int32, (32, F), 0)

    def place_cold(o, carry):
        rows = cold[o].astype(f32)
        live = slot_index < counts[o]
        table[pl.ds(pl.multiple_of(HOT_ROWS + o * 32, 32), 32), :] = jnp.where(live, rows, 0.0)
        return carry

    lax.fori_loop(0, 64, place_cold, 0, unroll=4)

    w1[0:F, :] = w1_self[...]
    w1[F : 2 * F, :] = w1_neigh[...]
    for padded, given in ((w2s, w2_self), (w2n, w2_neigh)):
        padded[...] = jnp.zeros((256, HID), bf16)
        padded[0:CLASSES, :] = given[...]
    hidden[...] = jnp.zeros((2 * SEEDS, HID), f32)

    def gather(chunk, buffer):
        base = chunk * STEP
        for u in range(STEP):
            m = base + u
            rows = [table[pl.ds(near[m], 1), :] for near in neighbours]
            buffer[u : u + 1, 0:F] = table[pl.ds(own[m], 1), :]
            buffer[u : u + 1, F : 2 * F] = tree_sum(rows)

    def forward(chunk, buffer):
        row = pl.multiple_of(chunk * STEP, STEP)
        x_all[pl.ds(row, STEP), 0:F] = buffer[:, 0:F].astype(bf16)
        x_all[pl.ds(row, STEP), F : 2 * F] = (buffer[:, F : 2 * F] * (1.0 / FAN0)).astype(bf16)
        x = jnp.concatenate(
            [buffer[:, 0:F].astype(bf16), (buffer[:, F : 2 * F] * (1.0 / FAN0)).astype(bf16)], axis=1
        )
        v = jnp.dot(x, w1[...], preferred_element_type=f32)
        square = v * v
        t = jnp.tanh(v * (GELU_C + (GELU_C * GELU_A) * square))
        half = 0.5 + 0.5 * t
        h = (v * half).astype(bf16).astype(f32)
        slope[pl.ds(row, STEP), :] = half + (0.5 * v) * (1.0 - t * t) * (
            GELU_C + (3.0 * GELU_C * GELU_A) * square
        )
        into = pl.multiple_of(
            lax.rem(chunk, SEED_CHUNKS) * STEP + jnp.where(chunk >= SEED_CHUNKS, SEEDS, 0), STEP
        )
        hidden[pl.ds(into, STEP), :] += h

    for copy in pieces[0]:
        copy.wait()
    gather(0, x_even)

    def two_chunks(i, carry):
        gather(2 * i + 1, x_odd)
        forward(2 * i, x_even)
        for p, start in enumerate(PIECES[1:-1]):

            @pl.when(2 * i + 2 == start // STEP)
            def _():
                for copy in pieces[p + 1]:
                    copy.wait()

        gather(lax.rem(2 * i + 2, CHUNKS), x_even)
        forward(2 * i + 1, x_odd)
        return carry

    lax.fori_loop(0, CHUNKS // 2, two_chunks, 0)

    hidden_b[0:SEEDS, :] = hidden[0:SEEDS, :].astype(bf16)
    hidden_b[SEEDS:, :] = (hidden[SEEDS:, :] / FAN1).astype(bf16)
    nt = (((1,), (1,)), ((), ()))
    tn = (((0,), (0,)), ((), ()))
    eye = lax.broadcasted_iota(jnp.int32, (128, 128), 0) == lax.broadcasted_iota(
        jnp.int32, (128, 128), 1
    )
    lane = lax.broadcasted_iota(jnp.int32, (128, 256), 1)
    for b in range(SEEDS // 128):
        rows = slice(b * 128, (b + 1) * 128)
        logits = lax.dot_general(
            hidden_b[rows, :], w2s[...], nt, preferred_element_type=f32
        ) + lax.dot_general(
            hidden_b[SEEDS + b * 128 : SEEDS + (b + 1) * 128, :], w2n[...], nt,
            preferred_element_type=f32,
        )
        label_row = labels[:, rows].astype(f32)
        label = jnp.sum(jnp.where(eye, label_row, 0.0), axis=1, keepdims=True).astype(jnp.int32)
        valid = lane < CLASSES
        top = jnp.max(jnp.where(valid, logits, -3.0e38), axis=1, keepdims=True)
        total = jnp.sum(jnp.where(valid, jnp.exp(logits - top), 0.0), axis=1, keepdims=True)
        log_total = jnp.log(total) + top
        hit = lane == label
        picked = jnp.sum(jnp.where(hit, logits, 0.0), axis=1, keepdims=True)
        loss = log_total - picked
        loss_out[:, rows] = jnp.sum(jnp.where(eye, loss, 0.0), axis=0, keepdims=True)
        probs = jnp.where(valid, jnp.exp(logits - log_total), 0.0)
        grad_logits[rows, :] = ((probs - hit.astype(f32)) / SEEDS).astype(bf16)

    left, right = core[0], 1 - core[0]
    g = grad_logits[...]
    terms[:, 608:, :] = jnp.zeros((2, HALF_ROWS - 608, F), f32)
    for at, part in ((256, slice(0, SEEDS)), (256 + CLASS_ROWS, slice(SEEDS, 2 * SEEDS))):
        term = lax.dot_general(g, hidden_b[part, :], tn, preferred_element_type=f32)
        terms[left, at : at + CLASS_ROWS, :] = term[0:CLASS_ROWS, 0:F]
        terms[right, at : at + CLASS_ROWS, :] = term[0:CLASS_ROWS, F:]
    back[0:SEEDS, :] = jnp.dot(g, w2s[...], preferred_element_type=f32)
    back[SEEDS:, :] = jnp.dot(g, w2n[...], preferred_element_type=f32) / FAN1

    def backward(j, into):
        row = pl.multiple_of(j * SEEDS, SEEDS)
        grad_pre = (slope[pl.ds(row, SEEDS), :] * back[into, :]).astype(bf16)
        return lax.dot_general(x_all[pl.ds(row, SEEDS), :], grad_pre, tn, preferred_element_type=f32)

    w1_acc[...] = backward(0, slice(0, SEEDS))

    def add_block(j, carry):
        terms_of = [backward(5 * j + 1 + i, slice(SEEDS, 2 * SEEDS)) for i in range(5)]
        w1_acc[...] += tree_sum(terms_of)
        return carry

    lax.fori_loop(0, FAN1 // 5, add_block, 0)
    terms[left, 0:256, :] = w1_acc[:, 0:F]
    terms[right, 0:256, :] = w1_acc[:, F:]
    keep_out[...] = terms[0]
    send_out[...] = terms[1]


def train(counts, where_hot, core, places, hot, cold, labels, w1_self, w1_neigh, w2_self_t, w2_neigh_t):
    smem = pl.BlockSpec(memory_space=pltpu.SMEM)
    vmem = pl.BlockSpec(memory_space=pltpu.VMEM)
    anywhere = pl.BlockSpec(memory_space=pl.ANY)
    return pl.pallas_call(
        train_kernel,
        out_shape=(
            jax.ShapeDtypeStruct((1, SEEDS), jnp.float32),
            jax.ShapeDtypeStruct((HALF_ROWS, F), jnp.float32),
            jax.ShapeDtypeStruct((HALF_ROWS, F), jnp.float32),
        ),
        in_specs=[smem] * 3 + [anywhere] + [vmem] * 10,
        out_specs=(vmem, vmem, vmem),
        scratch_shapes=[
            *[pltpu.SMEM((SLOTS,), jnp.int32) for _ in range(POSITIONS)],
            pltpu.SemaphoreType.DMA((len(PIECES) - 1, POSITIONS)),
            pltpu.VMEM((HOT_ROWS + COLD_ROWS, F), jnp.float32),
            pltpu.VMEM((STEP, 2 * F), jnp.float32),
            pltpu.VMEM((STEP, 2 * F), jnp.float32),
            pltpu.VMEM((2 * F, HID), jnp.bfloat16),
            pltpu.VMEM((256, HID), jnp.bfloat16),
            pltpu.VMEM((256, HID), jnp.bfloat16),
            pltpu.VMEM((SLOTS, 2 * F), jnp.bfloat16),
            pltpu.VMEM((SLOTS, HID), jnp.float32),
            pltpu.VMEM((2 * SEEDS, HID), jnp.float32),
            pltpu.VMEM((2 * SEEDS, HID), jnp.bfloat16),
            pltpu.VMEM((SEEDS, 256), jnp.bfloat16),
            pltpu.VMEM((2 * SEEDS, HID), jnp.float32),
            pltpu.VMEM((2 * F, HID), jnp.float32),
            pltpu.VMEM((2, HALF_ROWS, F), jnp.float32),
        ],
        compiler_params=pltpu.CompilerParams(vmem_limit_bytes=44 << 20),
        cost_estimate=pl.CostEstimate(flops=4 << 30, bytes_accessed=4 << 20, transcendentals=2 << 20),
        name="train",
    )(
        counts, where_hot, core, places, *hot, cold, labels, w1_self, w1_neigh, w2_self_t, w2_neigh_t,
    )


def pick_kernel(n, *refs):
    asked, shard, given = refs[:n], refs[n], refs[n + 1 : 2 * n + 1]
    narrow, wide, picked, copied = refs[2 * n + 1 :]
    step = shard.shape[0] // PARTS
    parts = [pl.ds(i * step, step) for i in range(PARTS)]
    copies = [
        pltpu.make_async_copy(shard.at[part], narrow.at[part], copied.at[i])
        for i, part in enumerate(parts)
    ]
    for copy in copies:
        copy.start()
    for copy, part in zip(copies, parts):
        copy.wait()
        wide[part, :] = narrow[part, :].astype(jnp.float32)
    row = 0
    for ids, out in zip(asked, given):
        first = row
        for at in np.ndindex(ids.shape):
            picked[row : row + 1, :] = wide[pl.ds(ids[at], 1), :]
            row += 1
        if len(out.shape) == 2:
            out[...] = picked[first:row, :].astype(out.dtype)
        else:
            size = out.shape[1]
            for o in range(out.shape[0]):
                out[o] = picked[first + o * size : first + (o + 1) * size, :].astype(out.dtype)


def pick_rows(shard, asked, name):
    n = len(asked)
    total = sum(int(np.prod(ids.shape)) for ids in asked)
    return pl.pallas_call(
        lambda *refs: pick_kernel(n, *refs),
        out_shape=tuple(jax.ShapeDtypeStruct(ids.shape + (F,), jnp.bfloat16) for ids in asked),
        in_specs=[pl.BlockSpec(memory_space=pltpu.SMEM)] * n + [pl.BlockSpec(memory_space=pltpu.HBM)],
        out_specs=tuple(pl.BlockSpec(memory_space=pltpu.VMEM) for _ in asked),
        scratch_shapes=[
            pltpu.VMEM(shard.shape, shard.dtype),
            pltpu.VMEM(shard.shape, jnp.float32),
            pltpu.VMEM((total, F), jnp.float32),
            pltpu.SemaphoreType.DMA((PARTS,)),
        ],
        compiler_params=pltpu.CompilerParams(vmem_limit_bytes=40 << 20),
        cost_estimate=pl.CostEstimate(flops=0, bytes_accessed=4 << 20, transcendentals=0),
        name=name,
    )(*asked, shard)


def clique_peers(hot_ids):
    me = lax.axis_index("clique")
    peers = [lax.rem(me + d, 4) for d in range(4)]
    return peers, [lax.dynamic_index_in_dim(hot_ids, peer, 0, keepdims=False) for peer in peers]


def send_hot(rows):
    return [rows[0]] + [
        lax.ppermute(rows[d], "clique", [(i, (i - d) % 4) for i in range(4)]) for d in (1, 2, 3)
    ]


def exchange(x, axes):
    return lax.all_to_all(x, axes, split_axis=0, concat_axis=0, tiled=True)


def share(x, axes, n):
    return exchange(jnp.broadcast_to(x[None], (n,) + x.shape), axes)


SWAP = [(0, 1), (1, 0)]


def split_kernel(core, mine, other, *outs):
    for first, at in ((0, slice(0, F)), (1, slice(F, 2 * F))):
        for out, row in zip(outs, (0, F, 2 * F, 2 * F + CLASS_ROWS)):
            rows = slice(row, row + out.shape[0])
            out[:, at] = jnp.where(core[0] == first, mine[rows, :], other[rows, :])


def sum_everywhere(keep, send, core):
    mine = keep + lax.ppermute(send, "core", SWAP)
    mine = exchange(mine.reshape(16, HALF_ROWS // 128, 8, F), ("clique", "y")).sum(0)
    mine = share(mine, "z", 8).sum(0)
    mine = share(mine, ("clique", "y"), 16).reshape(HALF_ROWS, F)
    other = lax.ppermute(mine, "core", SWAP)
    vmem = pl.BlockSpec(memory_space=pltpu.VMEM)
    return pl.pallas_call(
        split_kernel,
        out_shape=tuple(jax.ShapeDtypeStruct((n, HID), jnp.float32) for n in (F, F, CLASSES, CLASSES)),
        in_specs=[pl.BlockSpec(memory_space=pltpu.SMEM), vmem, vmem],
        out_specs=(vmem,) * 4,
        compiler_params=pltpu.CompilerParams(vmem_limit_bytes=8 << 20),
        name="split",
    )(core, mine, other)


def body(
    hot_shard, cold_shard, hot_ids, cold_ids, cold_counts, mid_self, nbr1, nbr2, labels,
    w1_self, w1_neigh, w2_self, w2_neigh,
):
    peers, hot_asked = clique_peers(hot_ids[0])
    hot_asked[1:] = [
        lax.ppermute(hot_asked[d], "clique", [(i, (i + d) % 4) for i in range(4)]) for d in (1, 2, 3)
    ]
    cold_asked = exchange(cold_ids[0], GROUP)
    *hot_asked, cold_asked = lax.optimization_barrier((*hot_asked, cold_asked))
    (served,) = pick_rows(cold_shard, [cold_asked], "pick_cold")
    cold = exchange(served, GROUP)
    *hot_asked, served = lax.optimization_barrier((*hot_asked, served))
    rows = pick_rows(hot_shard, hot_asked, "pick_hot")
    *rows, nbr2 = lax.optimization_barrier((*rows, nbr2))
    hot = send_hot(rows)
    places = order_positions(nbr1[0], nbr2[0], mid_self[0])
    core = lax.axis_index("core").astype(jnp.int32)[None]
    loss, keep, send = train(
        cold_counts[0], jnp.stack(peers).astype(jnp.int32), core, places,
        hot, cold, labels, w1_self, w1_neigh, w2_self.T, w2_neigh.T,
    )
    w1s, w1n, w2s, w2n = sum_everywhere(keep, send, core)
    return loss, w1s, w1n, w2s.T, w2n.T


def solution(mesh):
    mesh = Mesh(mesh.devices.reshape(4, 8, 4, 2), AXES)
    each = P(AXES)
    return jax.shard_map(
        body,
        mesh=mesh,
        in_specs=(P("clique"), P(GROUP)) + (each,) * 7 + (P(),) * 4,
        out_specs=(each, P(), P(), P(), P()),
        check_vma=False,
    )
```

```python
import jax
import jax.numpy as jnp
import numpy as np
from jax import lax
from jax.experimental import pallas as pl
from jax.experimental.pallas import tpu as pltpu
from jax.sharding import Mesh
from jax.sharding import PartitionSpec as P

AXES = ("clique", "z", "y", "core")
GROUP = ("z", "y", "core")
F = 128
HID = 256
CLASSES = 172
CLASS_ROWS = 176
SEEDS = 512
MID = 7680
FAN0 = 10
POSITIONS = FAN0 + 1
FAN1 = 15
HOT_ROWS = 2048
COLD_ROWS = 2048
STEP = 64
FIRST, SECOND = range(32), range(32, STEP)
SLOTS = SEEDS * (FAN1 + 1)
CHUNKS = SLOTS // STEP
SEED_CHUNKS = SEEDS // STEP
HALF_ROWS = 640
PARTS = 8
PIECES = (0, 512, 2048, SLOTS)
GELU_C = float(np.sqrt(2.0 / np.pi))
GELU_A = 0.044715


def tree_sum(rows):
    while len(rows) > 1:
        rows = [
            rows[i] + rows[i + 1] if i + 1 < len(rows) else rows[i]
            for i in range(0, len(rows), 2)
        ]
    return rows[0]


def order_kernel(nbr2, nbr1, mid_self, out, slots, info, ordered, copied):
    copies = [
        pltpu.make_async_copy(nbr2.at[k, 0], slots.at[pl.ds(k * SEEDS, SEEDS)], copied.at[k])
        for k in range(FAN1)
    ]
    for copy in copies:
        copy.start()
    empty = jnp.zeros((128 - POSITIONS, 128), jnp.int32)

    def by_node(i, carry):
        at = pl.ds(pl.multiple_of(i * 128, 128), 128)
        rows = [nbr1[k, :, at] for k in range(FAN0)] + [mid_self[:, at]]
        info[at, :] = jnp.concatenate([*rows, empty], axis=0).T
        return carry

    lax.fori_loop(0, MID // 128, by_node, 0, unroll=4)
    for k in range(FAN0):
        out[k, :, 0:SEEDS] = nbr1[k, :, 0:SEEDS]
    out[FAN0, :, 0:SEEDS] = mid_self[:, 0:SEEDS]
    for copy in copies:
        copy.wait()

    chunks = MID // 128

    def by_chunk(i, carry):
        before = jnp.maximum(i - 1, 0) * 128
        rows = ordered[pl.ds(pl.multiple_of(before, 128), 128), :].T
        base = jnp.minimum(i, chunks - 1) * 128
        for u in range(128):
            ordered[pl.ds(base + u, 1), :] = info[pl.ds(slots[base + u], 1), :]
        at = pl.ds(pl.multiple_of(SEEDS + before, 128), 128)
        for k in range(POSITIONS):
            out[k, :, at] = rows[k : k + 1, :]
        return carry

    lax.fori_loop(0, chunks + 1, by_chunk, 0)


def order_positions(nbr1, nbr2, mid_self):
    vmem = pl.BlockSpec(memory_space=pltpu.VMEM)
    return pl.pallas_call(
        order_kernel,
        out_shape=jax.ShapeDtypeStruct((POSITIONS, 1, SLOTS), jnp.int32),
        in_specs=[pl.BlockSpec(memory_space=pl.ANY), vmem, vmem],
        out_specs=vmem,
        scratch_shapes=[
            pltpu.SMEM((MID,), jnp.int32),
            pltpu.VMEM((MID, 128), jnp.int32),
            pltpu.VMEM((MID, 128), jnp.int32),
            pltpu.SemaphoreType.DMA((FAN1,)),
        ],
        compiler_params=pltpu.CompilerParams(vmem_limit_bytes=16 << 20),
        cost_estimate=pl.CostEstimate(flops=0, bytes_accessed=8 << 20, transcendentals=0),
        name="order",
    )(nbr2[:, None], nbr1[:, None], mid_self[None])


def train_kernel(
    counts, where_hot, core, places,
    hot0, hot1, hot2, hot3, cold, labels, w1_self, w1_neigh, w2_self, w2_neigh,
    loss_out, keep_out, send_out,
    n0, n1, n2, n3, n4, n5, n6, n7, n8, n9, own, copied,
    table, x_even, x_odd, w1, w2s, w2n, x_all, slope, hidden, hidden_b, grad_logits, back, w1_acc, terms,
):
    f32, bf16 = jnp.float32, jnp.bfloat16
    neighbours = (n0, n1, n2, n3, n4, n5, n6, n7, n8, n9)
    pieces = []
    for p, (start, stop) in enumerate(zip(PIECES[:-1], PIECES[1:])):
        at = pl.ds(start, stop - start)
        pieces.append(
            [
                pltpu.make_async_copy(places.at[k, 0, at], to.at[at], copied.at[p, k])
                for k, to in enumerate((*neighbours, own))
            ]
        )
    for copies in pieces:
        for copy in copies:
            copy.start()

    for d, block in enumerate((hot0, hot1, hot2, hot3)):
        start = pl.multiple_of(where_hot[d] * 512, 512)
        table[pl.ds(start, 512), :] = block[...].astype(f32)
    slot_index = lax.broadcasted_iota(jnp.int32, (32, F), 0)

    def place_cold(o, carry):
        rows = cold[o].astype(f32)
        live = slot_index < counts[o]
        table[pl.ds(pl.multiple_of(HOT_ROWS + o * 32, 32), 32), :] = jnp.where(live, rows, 0.0)
        return carry

    lax.fori_loop(0, 64, place_cold, 0, unroll=4)

    w1[0:F, :] = w1_self[...]
    w1[F : 2 * F, :] = w1_neigh[...]
    for padded, given in ((w2s, w2_self), (w2n, w2_neigh)):
        padded[...] = jnp.zeros((256, HID), bf16)
        padded[0:CLASSES, :] = given[...]
    hidden[...] = jnp.zeros((2 * SEEDS, HID), f32)

    def gather(chunk, buffer, part):
        base = chunk * STEP
        for u in part:
            m = base + u
            rows = [table[pl.ds(near[m], 1), :] for near in neighbours]
            buffer[u : u + 1, 0:F] = table[pl.ds(own[m], 1), :]
            buffer[u : u + 1, F : 2 * F] = tree_sum(rows)

    def forward(chunk, buffer):
        row = pl.multiple_of(chunk * STEP, STEP)
        x_all[pl.ds(row, STEP), 0:F] = buffer[:, 0:F].astype(bf16)
        x_all[pl.ds(row, STEP), F : 2 * F] = (buffer[:, F : 2 * F] * (1.0 / FAN0)).astype(bf16)
        x = jnp.concatenate(
            [buffer[:, 0:F].astype(bf16), (buffer[:, F : 2 * F] * (1.0 / FAN0)).astype(bf16)], axis=1
        )
        v = jnp.dot(x, w1[...], preferred_element_type=f32)
        square = v * v
        t = jnp.tanh(v * (GELU_C + (GELU_C * GELU_A) * square))
        half = 0.5 + 0.5 * t
        h = (v * half).astype(bf16).astype(f32)
        slope[pl.ds(row, STEP), :] = half + (0.5 * v) * (1.0 - t * t) * (
            GELU_C + (3.0 * GELU_C * GELU_A) * square
        )
        into = pl.multiple_of(
            lax.rem(chunk, SEED_CHUNKS) * STEP + jnp.where(chunk >= SEED_CHUNKS, SEEDS, 0), STEP
        )
        hidden[pl.ds(into, STEP), :] += h

    for copy in pieces[0]:
        copy.wait()
    gather(0, x_even, range(STEP))

    def two_chunks(i, carry):
        gather(2 * i + 1, x_odd, FIRST)
        forward(2 * i, x_even)
        gather(2 * i + 1, x_odd, SECOND)
        for p, start in enumerate(PIECES[1:-1]):

            @pl.when(2 * i + 2 == start // STEP)
            def _():
                for copy in pieces[p + 1]:
                    copy.wait()

        gather(lax.rem(2 * i + 2, CHUNKS), x_even, FIRST)
        forward(2 * i + 1, x_odd)
        gather(lax.rem(2 * i + 2, CHUNKS), x_even, SECOND)
        return carry

    lax.fori_loop(0, CHUNKS // 2, two_chunks, 0)

    hidden_b[0:SEEDS, :] = hidden[0:SEEDS, :].astype(bf16)
    hidden_b[SEEDS:, :] = (hidden[SEEDS:, :] / FAN1).astype(bf16)
    nt = (((1,), (1,)), ((), ()))
    tn = (((0,), (0,)), ((), ()))
    eye = lax.broadcasted_iota(jnp.int32, (128, 128), 0) == lax.broadcasted_iota(
        jnp.int32, (128, 128), 1
    )
    lane = lax.broadcasted_iota(jnp.int32, (128, 256), 1)
    for b in range(SEEDS // 128):
        rows = slice(b * 128, (b + 1) * 128)
        logits = lax.dot_general(
            hidden_b[rows, :], w2s[...], nt, preferred_element_type=f32
        ) + lax.dot_general(
            hidden_b[SEEDS + b * 128 : SEEDS + (b + 1) * 128, :], w2n[...], nt,
            preferred_element_type=f32,
        )
        label_row = labels[:, rows].astype(f32)
        label = jnp.sum(jnp.where(eye, label_row, 0.0), axis=1, keepdims=True).astype(jnp.int32)
        valid = lane < CLASSES
        top = jnp.max(jnp.where(valid, logits, -3.0e38), axis=1, keepdims=True)
        total = jnp.sum(jnp.where(valid, jnp.exp(logits - top), 0.0), axis=1, keepdims=True)
        log_total = jnp.log(total) + top
        hit = lane == label
        picked = jnp.sum(jnp.where(hit, logits, 0.0), axis=1, keepdims=True)
        loss = log_total - picked
        loss_out[:, rows] = jnp.sum(jnp.where(eye, loss, 0.0), axis=0, keepdims=True)
        probs = jnp.where(valid, jnp.exp(logits - log_total), 0.0)
        grad_logits[rows, :] = ((probs - hit.astype(f32)) / SEEDS).astype(bf16)

    left, right = core[0], 1 - core[0]
    g = grad_logits[...]
    terms[:, 608:, :] = jnp.zeros((2, HALF_ROWS - 608, F), f32)
    for at, part in ((256, slice(0, SEEDS)), (256 + CLASS_ROWS, slice(SEEDS, 2 * SEEDS))):
        term = lax.dot_general(g, hidden_b[part, :], tn, preferred_element_type=f32)
        terms[left, at : at + CLASS_ROWS, :] = term[0:CLASS_ROWS, 0:F]
        terms[right, at : at + CLASS_ROWS, :] = term[0:CLASS_ROWS, F:]
    back[0:SEEDS, :] = jnp.dot(g, w2s[...], preferred_element_type=f32)
    back[SEEDS:, :] = jnp.dot(g, w2n[...], preferred_element_type=f32) / FAN1

    def backward(j, into):
        row = pl.multiple_of(j * SEEDS, SEEDS)
        grad_pre = (slope[pl.ds(row, SEEDS), :] * back[into, :]).astype(bf16)
        return lax.dot_general(x_all[pl.ds(row, SEEDS), :], grad_pre, tn, preferred_element_type=f32)

    w1_acc[...] = backward(0, slice(0, SEEDS))

    def add_block(j, carry):
        terms_of = [backward(5 * j + 1 + i, slice(SEEDS, 2 * SEEDS)) for i in range(5)]
        w1_acc[...] += tree_sum(terms_of)
        return carry

    lax.fori_loop(0, FAN1 // 5, add_block, 0)
    terms[left, 0:256, :] = w1_acc[:, 0:F]
    terms[right, 0:256, :] = w1_acc[:, F:]
    keep_out[...] = terms[0]
    send_out[...] = terms[1]


def train(counts, where_hot, core, places, hot, cold, labels, w1_self, w1_neigh, w2_self_t, w2_neigh_t):
    smem = pl.BlockSpec(memory_space=pltpu.SMEM)
    vmem = pl.BlockSpec(memory_space=pltpu.VMEM)
    anywhere = pl.BlockSpec(memory_space=pl.ANY)
    return pl.pallas_call(
        train_kernel,
        out_shape=(
            jax.ShapeDtypeStruct((1, SEEDS), jnp.float32),
            jax.ShapeDtypeStruct((HALF_ROWS, F), jnp.float32),
            jax.ShapeDtypeStruct((HALF_ROWS, F), jnp.float32),
        ),
        in_specs=[smem] * 3 + [anywhere] + [vmem] * 10,
        out_specs=(vmem, vmem, vmem),
        scratch_shapes=[
            *[pltpu.SMEM((SLOTS,), jnp.int32) for _ in range(POSITIONS)],
            pltpu.SemaphoreType.DMA((len(PIECES) - 1, POSITIONS)),
            pltpu.VMEM((HOT_ROWS + COLD_ROWS, F), jnp.float32),
            pltpu.VMEM((STEP, 2 * F), jnp.float32),
            pltpu.VMEM((STEP, 2 * F), jnp.float32),
            pltpu.VMEM((2 * F, HID), jnp.bfloat16),
            pltpu.VMEM((256, HID), jnp.bfloat16),
            pltpu.VMEM((256, HID), jnp.bfloat16),
            pltpu.VMEM((SLOTS, 2 * F), jnp.bfloat16),
            pltpu.VMEM((SLOTS, HID), jnp.float32),
            pltpu.VMEM((2 * SEEDS, HID), jnp.float32),
            pltpu.VMEM((2 * SEEDS, HID), jnp.bfloat16),
            pltpu.VMEM((SEEDS, 256), jnp.bfloat16),
            pltpu.VMEM((2 * SEEDS, HID), jnp.float32),
            pltpu.VMEM((2 * F, HID), jnp.float32),
            pltpu.VMEM((2, HALF_ROWS, F), jnp.float32),
        ],
        compiler_params=pltpu.CompilerParams(vmem_limit_bytes=44 << 20),
        cost_estimate=pl.CostEstimate(flops=4 << 30, bytes_accessed=4 << 20, transcendentals=2 << 20),
        name="train",
    )(
        counts, where_hot, core, places, *hot, cold, labels, w1_self, w1_neigh, w2_self_t, w2_neigh_t,
    )


def pick_kernel(n, *refs):
    asked, shard, given = refs[:n], refs[n], refs[n + 1 : 2 * n + 1]
    narrow, wide, picked, copied = refs[2 * n + 1 :]
    step = shard.shape[0] // PARTS
    parts = [pl.ds(i * step, step) for i in range(PARTS)]
    copies = [
        pltpu.make_async_copy(shard.at[part], narrow.at[part], copied.at[i])
        for i, part in enumerate(parts)
    ]
    for copy in copies:
        copy.start()
    for copy, part in zip(copies, parts):
        copy.wait()
        wide[part, :] = narrow[part, :].astype(jnp.float32)
    row = 0
    for ids, out in zip(asked, given):
        first = row
        for at in np.ndindex(ids.shape):
            picked[row : row + 1, :] = wide[pl.ds(ids[at], 1), :]
            row += 1
        if len(out.shape) == 2:
            out[...] = picked[first:row, :].astype(out.dtype)
        else:
            size = out.shape[1]
            for o in range(out.shape[0]):
                out[o] = picked[first + o * size : first + (o + 1) * size, :].astype(out.dtype)


def pick_rows(shard, asked, name):
    n = len(asked)
    total = sum(int(np.prod(ids.shape)) for ids in asked)
    return pl.pallas_call(
        lambda *refs: pick_kernel(n, *refs),
        out_shape=tuple(jax.ShapeDtypeStruct(ids.shape + (F,), jnp.bfloat16) for ids in asked),
        in_specs=[pl.BlockSpec(memory_space=pltpu.SMEM)] * n + [pl.BlockSpec(memory_space=pltpu.HBM)],
        out_specs=tuple(pl.BlockSpec(memory_space=pltpu.VMEM) for _ in asked),
        scratch_shapes=[
            pltpu.VMEM(shard.shape, shard.dtype),
            pltpu.VMEM(shard.shape, jnp.float32),
            pltpu.VMEM((total, F), jnp.float32),
            pltpu.SemaphoreType.DMA((PARTS,)),
        ],
        compiler_params=pltpu.CompilerParams(vmem_limit_bytes=40 << 20),
        cost_estimate=pl.CostEstimate(flops=0, bytes_accessed=4 << 20, transcendentals=0),
        name=name,
    )(*asked, shard)


def clique_peers(hot_ids):
    me = lax.axis_index("clique")
    peers = [lax.rem(me + d, 4) for d in range(4)]
    return peers, [lax.dynamic_index_in_dim(hot_ids, peer, 0, keepdims=False) for peer in peers]


def send_hot(rows):
    return [rows[0]] + [
        lax.ppermute(rows[d], "clique", [(i, (i - d) % 4) for i in range(4)]) for d in (1, 2, 3)
    ]


def exchange(x, axes):
    return lax.all_to_all(x, axes, split_axis=0, concat_axis=0, tiled=True)


def share(x, axes, n):
    return exchange(jnp.broadcast_to(x[None], (n,) + x.shape), axes)


SWAP = [(0, 1), (1, 0)]


def split_kernel(core, mine, other, *outs):
    for first, at in ((0, slice(0, F)), (1, slice(F, 2 * F))):
        for out, row in zip(outs, (0, F, 2 * F, 2 * F + CLASS_ROWS)):
            rows = slice(row, row + out.shape[0])
            out[:, at] = jnp.where(core[0] == first, mine[rows, :], other[rows, :])


def sum_everywhere(keep, send, core):
    mine = keep + lax.ppermute(send, "core", SWAP)
    mine = exchange(mine.reshape(16, HALF_ROWS // 128, 8, F), ("clique", "y")).sum(0)
    mine = share(mine, "z", 8).sum(0)
    mine = share(mine, ("clique", "y"), 16).reshape(HALF_ROWS, F)
    other = lax.ppermute(mine, "core", SWAP)
    vmem = pl.BlockSpec(memory_space=pltpu.VMEM)
    return pl.pallas_call(
        split_kernel,
        out_shape=tuple(jax.ShapeDtypeStruct((n, HID), jnp.float32) for n in (F, F, CLASSES, CLASSES)),
        in_specs=[pl.BlockSpec(memory_space=pltpu.SMEM), vmem, vmem],
        out_specs=(vmem,) * 4,
        compiler_params=pltpu.CompilerParams(vmem_limit_bytes=8 << 20),
        name="split",
    )(core, mine, other)


def body(
    hot_shard, cold_shard, hot_ids, cold_ids, cold_counts, mid_self, nbr1, nbr2, labels,
    w1_self, w1_neigh, w2_self, w2_neigh,
):
    peers, hot_asked = clique_peers(hot_ids[0])
    hot_asked[1:] = [
        lax.ppermute(hot_asked[d], "clique", [(i, (i + d) % 4) for i in range(4)]) for d in (1, 2, 3)
    ]
    cold_asked = exchange(cold_ids[0], GROUP)
    *hot_asked, cold_asked = lax.optimization_barrier((*hot_asked, cold_asked))
    (served,) = pick_rows(cold_shard, [cold_asked], "pick_cold")
    cold = exchange(served, GROUP)
    *hot_asked, served = lax.optimization_barrier((*hot_asked, served))
    rows = pick_rows(hot_shard, hot_asked, "pick_hot")
    *rows, nbr2 = lax.optimization_barrier((*rows, nbr2))
    hot = send_hot(rows)
    places = order_positions(nbr1[0], nbr2[0], mid_self[0])
    core = lax.axis_index("core").astype(jnp.int32)[None]
    loss, keep, send = train(
        cold_counts[0], jnp.stack(peers).astype(jnp.int32), core, places,
        hot, cold, labels, w1_self, w1_neigh, w2_self.T, w2_neigh.T,
    )
    w1s, w1n, w2s, w2n = sum_everywhere(keep, send, core)
    return loss, w1s, w1n, w2s.T, w2n.T


def solution(mesh):
    mesh = Mesh(mesh.devices.reshape(4, 8, 4, 2), AXES)
    each = P(AXES)
    return jax.shard_map(
        body,
        mesh=mesh,
        in_specs=(P("clique"), P(GROUP)) + (each,) * 7 + (P(),) * 4,
        out_specs=(each, P(), P(), P(), P()),
        check_vma=False,
    )
```

```python
import jax
import jax.numpy as jnp
import numpy as np
from jax import lax
from jax.experimental import pallas as pl
from jax.experimental.pallas import tpu as pltpu
from jax.sharding import Mesh
from jax.sharding import PartitionSpec as P

AXES = ("clique", "z", "y", "core")
GROUP = ("z", "y", "core")
F = 128
HID = 256
CLASSES = 172
CLASS_ROWS = 176
SEEDS = 512
MID = 7680
FAN0 = 10
POSITIONS = FAN0 + 1
FAN1 = 15
HOT_ROWS = 2048
COLD_ROWS = 2048
STEP = 64
FIRST, SECOND = range(32), range(32, STEP)
SLOTS = SEEDS * (FAN1 + 1)
CHUNKS = SLOTS // STEP
SEED_CHUNKS = SEEDS // STEP
HALF_ROWS = 640
PARTS = 8
PIECES = (0, 128, 1024, SLOTS)
GELU_C = float(np.sqrt(2.0 / np.pi))
GELU_A = 0.044715


def tree_sum(rows):
    while len(rows) > 1:
        rows = [
            rows[i] + rows[i + 1] if i + 1 < len(rows) else rows[i]
            for i in range(0, len(rows), 2)
        ]
    return rows[0]


def order_kernel(nbr2, nbr1, mid_self, out, slots, info, ordered, copied):
    copies = [
        pltpu.make_async_copy(nbr2.at[k, 0], slots.at[pl.ds(k * SEEDS, SEEDS)], copied.at[k])
        for k in range(FAN1)
    ]
    for copy in copies:
        copy.start()
    empty = jnp.zeros((128 - POSITIONS, 128), jnp.int32)

    def by_node(i, carry):
        at = pl.ds(pl.multiple_of(i * 128, 128), 128)
        rows = [nbr1[k, :, at] for k in range(FAN0)] + [mid_self[:, at]]
        info[at, :] = jnp.concatenate([*rows, empty], axis=0).T
        return carry

    lax.fori_loop(0, MID // 128, by_node, 0, unroll=4)
    for k in range(FAN0):
        out[k, :, 0:SEEDS] = nbr1[k, :, 0:SEEDS]
    out[FAN0, :, 0:SEEDS] = mid_self[:, 0:SEEDS]
    for copy in copies:
        copy.wait()

    chunks = MID // 128

    def by_chunk(i, carry):
        before = jnp.maximum(i - 1, 0) * 128
        rows = ordered[pl.ds(pl.multiple_of(before, 128), 128), :].T
        base = jnp.minimum(i, chunks - 1) * 128
        for u in range(128):
            ordered[pl.ds(base + u, 1), :] = info[pl.ds(slots[base + u], 1), :]
        at = pl.ds(pl.multiple_of(SEEDS + before, 128), 128)
        for k in range(POSITIONS):
            out[k, :, at] = rows[k : k + 1, :]
        return carry

    lax.fori_loop(0, chunks + 1, by_chunk, 0)


def order_positions(nbr1, nbr2, mid_self):
    vmem = pl.BlockSpec(memory_space=pltpu.VMEM)
    return pl.pallas_call(
        order_kernel,
        out_shape=jax.ShapeDtypeStruct((POSITIONS, 1, SLOTS), jnp.int32),
        in_specs=[pl.BlockSpec(memory_space=pl.ANY), vmem, vmem],
        out_specs=vmem,
        scratch_shapes=[
            pltpu.SMEM((MID,), jnp.int32),
            pltpu.VMEM((MID, 128), jnp.int32),
            pltpu.VMEM((MID, 128), jnp.int32),
            pltpu.SemaphoreType.DMA((FAN1,)),
        ],
        compiler_params=pltpu.CompilerParams(vmem_limit_bytes=16 << 20),
        cost_estimate=pl.CostEstimate(flops=0, bytes_accessed=8 << 20, transcendentals=0),
        name="order",
    )(nbr2[:, None], nbr1[:, None], mid_self[None])


def train_kernel(
    counts, where_hot, core, places,
    hot0, hot1, hot2, hot3, cold, labels, w1_self, w1_neigh, w2_self, w2_neigh,
    loss_out, keep_out, send_out,
    n0, n1, n2, n3, n4, n5, n6, n7, n8, n9, own, copied,
    table, x_even, x_odd, w1, w2s, w2n, x_all, slope, hidden, hidden_b, grad_logits, back, w1_acc, terms,
):
    f32, bf16 = jnp.float32, jnp.bfloat16
    neighbours = (n0, n1, n2, n3, n4, n5, n6, n7, n8, n9)
    pieces = []
    for p, (start, stop) in enumerate(zip(PIECES[:-1], PIECES[1:])):
        at = pl.ds(start, stop - start)
        pieces.append(
            [
                pltpu.make_async_copy(places.at[k, 0, at], to.at[at], copied.at[p, k])
                for k, to in enumerate((*neighbours, own))
            ]
        )
    for copies in pieces:
        for copy in copies:
            copy.start()

    for d, block in enumerate((hot0, hot1, hot2, hot3)):
        start = pl.multiple_of(where_hot[d] * 512, 512)
        table[pl.ds(start, 512), :] = block[...].astype(f32)
    slot_index = lax.broadcasted_iota(jnp.int32, (32, F), 0)

    def place_cold(o, carry):
        rows = cold[o].astype(f32)
        live = slot_index < counts[o]
        table[pl.ds(pl.multiple_of(HOT_ROWS + o * 32, 32), 32), :] = jnp.where(live, rows, 0.0)
        return carry

    lax.fori_loop(0, 64, place_cold, 0, unroll=4)

    w1[0:F, :] = w1_self[...]
    w1[F : 2 * F, :] = w1_neigh[...]
    for padded, given in ((w2s, w2_self), (w2n, w2_neigh)):
        padded[...] = jnp.zeros((256, HID), bf16)
        padded[0:CLASSES, :] = given[...]
    hidden[...] = jnp.zeros((2 * SEEDS, HID), f32)

    def gather(chunk, buffer, part):
        base = chunk * STEP
        for u in part:
            m = base + u
            rows = [table[pl.ds(near[m], 1), :] for near in neighbours]
            buffer[u : u + 1, 0:F] = table[pl.ds(own[m], 1), :]
            buffer[u : u + 1, F : 2 * F] = tree_sum(rows)

    def forward(chunk, buffer):
        row = pl.multiple_of(chunk * STEP, STEP)
        x_all[pl.ds(row, STEP), 0:F] = buffer[:, 0:F].astype(bf16)
        x_all[pl.ds(row, STEP), F : 2 * F] = (buffer[:, F : 2 * F] * (1.0 / FAN0)).astype(bf16)
        x = jnp.concatenate(
            [buffer[:, 0:F].astype(bf16), (buffer[:, F : 2 * F] * (1.0 / FAN0)).astype(bf16)], axis=1
        )
        v = jnp.dot(x, w1[...], preferred_element_type=f32)
        square = v * v
        t = jnp.tanh(v * (GELU_C + (GELU_C * GELU_A) * square))
        half = 0.5 + 0.5 * t
        h = (v * half).astype(bf16).astype(f32)
        slope[pl.ds(row, STEP), :] = half + (0.5 * v) * (1.0 - t * t) * (
            GELU_C + (3.0 * GELU_C * GELU_A) * square
        )
        into = pl.multiple_of(
            lax.rem(chunk, SEED_CHUNKS) * STEP + jnp.where(chunk >= SEED_CHUNKS, SEEDS, 0), STEP
        )
        hidden[pl.ds(into, STEP), :] += h

    for copy in pieces[0]:
        copy.wait()
    gather(0, x_even, range(STEP))

    def two_chunks(i, carry):
        gather(2 * i + 1, x_odd, FIRST)
        forward(2 * i, x_even)
        gather(2 * i + 1, x_odd, SECOND)
        for p, start in enumerate(PIECES[1:-1]):

            @pl.when(2 * i + 2 == start // STEP)
            def _():
                for copy in pieces[p + 1]:
                    copy.wait()

        gather(lax.rem(2 * i + 2, CHUNKS), x_even, FIRST)
        forward(2 * i + 1, x_odd)
        gather(lax.rem(2 * i + 2, CHUNKS), x_even, SECOND)
        return carry

    lax.fori_loop(0, CHUNKS // 2, two_chunks, 0)

    hidden_b[0:SEEDS, :] = hidden[0:SEEDS, :].astype(bf16)
    hidden_b[SEEDS:, :] = (hidden[SEEDS:, :] / FAN1).astype(bf16)
    nt = (((1,), (1,)), ((), ()))
    tn = (((0,), (0,)), ((), ()))
    eye = lax.broadcasted_iota(jnp.int32, (128, 128), 0) == lax.broadcasted_iota(
        jnp.int32, (128, 128), 1
    )
    lane = lax.broadcasted_iota(jnp.int32, (128, 256), 1)
    for b in range(SEEDS // 128):
        rows = slice(b * 128, (b + 1) * 128)
        logits = lax.dot_general(
            hidden_b[rows, :], w2s[...], nt, preferred_element_type=f32
        ) + lax.dot_general(
            hidden_b[SEEDS + b * 128 : SEEDS + (b + 1) * 128, :], w2n[...], nt,
            preferred_element_type=f32,
        )
        label_row = labels[:, rows].astype(f32)
        label = jnp.sum(jnp.where(eye, label_row, 0.0), axis=1, keepdims=True).astype(jnp.int32)
        valid = lane < CLASSES
        top = jnp.max(jnp.where(valid, logits, -3.0e38), axis=1, keepdims=True)
        total = jnp.sum(jnp.where(valid, jnp.exp(logits - top), 0.0), axis=1, keepdims=True)
        log_total = jnp.log(total) + top
        hit = lane == label
        picked = jnp.sum(jnp.where(hit, logits, 0.0), axis=1, keepdims=True)
        loss = log_total - picked
        loss_out[:, rows] = jnp.sum(jnp.where(eye, loss, 0.0), axis=0, keepdims=True)
        probs = jnp.where(valid, jnp.exp(logits - log_total), 0.0)
        grad_logits[rows, :] = ((probs - hit.astype(f32)) / SEEDS).astype(bf16)

    left, right = core[0], 1 - core[0]
    g = grad_logits[...]
    terms[:, 608:, :] = jnp.zeros((2, HALF_ROWS - 608, F), f32)
    for at, part in ((256, slice(0, SEEDS)), (256 + CLASS_ROWS, slice(SEEDS, 2 * SEEDS))):
        term = lax.dot_general(g, hidden_b[part, :], tn, preferred_element_type=f32)
        terms[left, at : at + CLASS_ROWS, :] = term[0:CLASS_ROWS, 0:F]
        terms[right, at : at + CLASS_ROWS, :] = term[0:CLASS_ROWS, F:]
    back[0:SEEDS, :] = jnp.dot(g, w2s[...], preferred_element_type=f32)
    back[SEEDS:, :] = jnp.dot(g, w2n[...], preferred_element_type=f32) / FAN1

    def backward(j, into):
        row = pl.multiple_of(j * SEEDS, SEEDS)
        grad_pre = (slope[pl.ds(row, SEEDS), :] * back[into, :]).astype(bf16)
        return lax.dot_general(x_all[pl.ds(row, SEEDS), :], grad_pre, tn, preferred_element_type=f32)

    w1_acc[...] = backward(0, slice(0, SEEDS))

    def add_block(j, carry):
        terms_of = [backward(5 * j + 1 + i, slice(SEEDS, 2 * SEEDS)) for i in range(5)]
        w1_acc[...] += tree_sum(terms_of)
        return carry

    lax.fori_loop(0, FAN1 // 5, add_block, 0)
    terms[left, 0:256, :] = w1_acc[:, 0:F]
    terms[right, 0:256, :] = w1_acc[:, F:]
    keep_out[...] = terms[0]
    send_out[...] = terms[1]


def train(counts, where_hot, core, places, hot, cold, labels, w1_self, w1_neigh, w2_self_t, w2_neigh_t):
    smem = pl.BlockSpec(memory_space=pltpu.SMEM)
    vmem = pl.BlockSpec(memory_space=pltpu.VMEM)
    anywhere = pl.BlockSpec(memory_space=pl.ANY)
    return pl.pallas_call(
        train_kernel,
        out_shape=(
            jax.ShapeDtypeStruct((1, SEEDS), jnp.float32),
            jax.ShapeDtypeStruct((HALF_ROWS, F), jnp.float32),
            jax.ShapeDtypeStruct((HALF_ROWS, F), jnp.float32),
        ),
        in_specs=[smem] * 3 + [anywhere] + [vmem] * 10,
        out_specs=(vmem, vmem, vmem),
        scratch_shapes=[
            *[pltpu.SMEM((SLOTS,), jnp.int32) for _ in range(POSITIONS)],
            pltpu.SemaphoreType.DMA((len(PIECES) - 1, POSITIONS)),
            pltpu.VMEM((HOT_ROWS + COLD_ROWS, F), jnp.float32),
            pltpu.VMEM((STEP, 2 * F), jnp.float32),
            pltpu.VMEM((STEP, 2 * F), jnp.float32),
            pltpu.VMEM((2 * F, HID), jnp.bfloat16),
            pltpu.VMEM((256, HID), jnp.bfloat16),
            pltpu.VMEM((256, HID), jnp.bfloat16),
            pltpu.VMEM((SLOTS, 2 * F), jnp.bfloat16),
            pltpu.VMEM((SLOTS, HID), jnp.float32),
            pltpu.VMEM((2 * SEEDS, HID), jnp.float32),
            pltpu.VMEM((2 * SEEDS, HID), jnp.bfloat16),
            pltpu.VMEM((SEEDS, 256), jnp.bfloat16),
            pltpu.VMEM((2 * SEEDS, HID), jnp.float32),
            pltpu.VMEM((2 * F, HID), jnp.float32),
            pltpu.VMEM((2, HALF_ROWS, F), jnp.float32),
        ],
        compiler_params=pltpu.CompilerParams(vmem_limit_bytes=44 << 20),
        cost_estimate=pl.CostEstimate(flops=4 << 30, bytes_accessed=4 << 20, transcendentals=2 << 20),
        name="train",
    )(
        counts, where_hot, core, places, *hot, cold, labels, w1_self, w1_neigh, w2_self_t, w2_neigh_t,
    )


def pick_kernel(n, *refs):
    asked, shard, given = refs[:n], refs[n], refs[n + 1 : 2 * n + 1]
    wide, picked = refs[2 * n + 1 :]
    step = shard.shape[0] // PARTS
    for i in range(PARTS):
        part = pl.ds(i * step, step)
        wide[part, :] = shard[part, :].astype(jnp.float32)
    row = 0
    for ids, out in zip(asked, given):
        first = row
        for at in np.ndindex(ids.shape):
            picked[row : row + 1, :] = wide[pl.ds(ids[at], 1), :]
            row += 1
        if len(out.shape) == 2:
            out[...] = picked[first:row, :].astype(out.dtype)
        else:
            size = out.shape[1]
            for o in range(out.shape[0]):
                out[o] = picked[first + o * size : first + (o + 1) * size, :].astype(out.dtype)


def pick_rows(shard, asked, name):
    n = len(asked)
    total = sum(int(np.prod(ids.shape)) for ids in asked)
    return pl.pallas_call(
        lambda *refs: pick_kernel(n, *refs),
        out_shape=tuple(jax.ShapeDtypeStruct(ids.shape + (F,), jnp.bfloat16) for ids in asked),
        in_specs=[pl.BlockSpec(memory_space=pltpu.SMEM)] * n + [pl.BlockSpec(memory_space=pltpu.VMEM)],
        out_specs=tuple(pl.BlockSpec(memory_space=pltpu.VMEM) for _ in asked),
        scratch_shapes=[
            pltpu.VMEM(shard.shape, jnp.float32),
            pltpu.VMEM((total, F), jnp.float32),
        ],
        compiler_params=pltpu.CompilerParams(vmem_limit_bytes=24 << 20),
        cost_estimate=pl.CostEstimate(flops=0, bytes_accessed=4 << 20, transcendentals=0),
        name=name,
    )(*asked, shard)


def clique_peers(hot_ids):
    me = lax.axis_index("clique")
    peers = [lax.rem(me + d, 4) for d in range(4)]
    return peers, [lax.dynamic_index_in_dim(hot_ids, peer, 0, keepdims=False) for peer in peers]


def send_hot(rows):
    return [rows[0]] + [
        lax.ppermute(rows[d], "clique", [(i, (i - d) % 4) for i in range(4)]) for d in (1, 2, 3)
    ]


def exchange(x, axes):
    return lax.all_to_all(x, axes, split_axis=0, concat_axis=0, tiled=True)


def share(x, axes, n):
    return exchange(jnp.broadcast_to(x[None], (n,) + x.shape), axes)


SWAP = [(0, 1), (1, 0)]


def split_kernel(core, mine, other, *outs):
    for first, at in ((0, slice(0, F)), (1, slice(F, 2 * F))):
        for out, row in zip(outs, (0, F, 2 * F, 2 * F + CLASS_ROWS)):
            rows = slice(row, row + out.shape[0])
            out[:, at] = jnp.where(core[0] == first, mine[rows, :], other[rows, :])


def sum_everywhere(keep, send, core):
    mine = keep + lax.ppermute(send, "core", SWAP)
    mine = exchange(mine.reshape(16, HALF_ROWS // 128, 8, F), ("clique", "y")).sum(0)
    mine = share(mine, "z", 8).sum(0)
    mine = share(mine, ("clique", "y"), 16).reshape(HALF_ROWS, F)
    other = lax.ppermute(mine, "core", SWAP)
    vmem = pl.BlockSpec(memory_space=pltpu.VMEM)
    return pl.pallas_call(
        split_kernel,
        out_shape=tuple(jax.ShapeDtypeStruct((n, HID), jnp.float32) for n in (F, F, CLASSES, CLASSES)),
        in_specs=[pl.BlockSpec(memory_space=pltpu.SMEM), vmem, vmem],
        out_specs=(vmem,) * 4,
        compiler_params=pltpu.CompilerParams(vmem_limit_bytes=8 << 20),
        name="split",
    )(core, mine, other)


def body(
    hot_shard, cold_shard, hot_ids, cold_ids, cold_counts, mid_self, nbr1, nbr2, labels,
    w1_self, w1_neigh, w2_self, w2_neigh,
):
    peers, hot_asked = clique_peers(hot_ids[0])
    hot_asked[1:] = [
        lax.ppermute(hot_asked[d], "clique", [(i, (i + d) % 4) for i in range(4)]) for d in (1, 2, 3)
    ]
    cold_asked = exchange(cold_ids[0], GROUP)
    *hot_asked, cold_asked = lax.optimization_barrier((*hot_asked, cold_asked))
    (served,) = pick_rows(cold_shard, [cold_asked], "pick_cold")
    cold = exchange(served, GROUP)
    *hot_asked, served = lax.optimization_barrier((*hot_asked, served))
    rows = pick_rows(hot_shard, hot_asked, "pick_hot")
    *rows, nbr2 = lax.optimization_barrier((*rows, nbr2))
    hot = send_hot(rows)
    places = order_positions(nbr1[0], nbr2[0], mid_self[0])
    core = lax.axis_index("core").astype(jnp.int32)[None]
    loss, keep, send = train(
        cold_counts[0], jnp.stack(peers).astype(jnp.int32), core, places,
        hot, cold, labels, w1_self, w1_neigh, w2_self.T, w2_neigh.T,
    )
    w1s, w1n, w2s, w2n = sum_everywhere(keep, send, core)
    return loss, w1s, w1n, w2s.T, w2n.T


def solution(mesh):
    mesh = Mesh(mesh.devices.reshape(4, 8, 4, 2), AXES)
    each = P(AXES)
    return jax.shard_map(
        body,
        mesh=mesh,
        in_specs=(P("clique"), P(GROUP)) + (each,) * 7 + (P(),) * 4,
        out_specs=(each, P(), P(), P(), P()),
        check_vma=False,
    )
```

```python
import jax
import jax.numpy as jnp
import numpy as np
from jax import lax
from jax.experimental import pallas as pl
from jax.experimental.pallas import tpu as pltpu
from jax.sharding import Mesh
from jax.sharding import PartitionSpec as P

AXES = ("clique", "z", "y", "core")
GROUP = ("z", "y", "core")
F = 128
HID = 256
CLASSES = 172
CLASS_ROWS = 176
SEEDS = 512
MID = 7680
FAN0 = 10
POSITIONS = FAN0 + 1
FAN1 = 15
HOT_ROWS = 2048
COLD_ROWS = 2048
STEP = 64
FIRST, SECOND = range(32), range(32, STEP)
SLOTS = SEEDS * (FAN1 + 1)
CHUNKS = SLOTS // STEP
SEED_CHUNKS = SEEDS // STEP
HALF_ROWS = 640
PARTS = 8
PIECES = (0, 128, 1024, SLOTS)
GELU_C = float(np.sqrt(2.0 / np.pi))
GELU_A = 0.044715


def tree_sum(rows):
    while len(rows) > 1:
        rows = [
            rows[i] + rows[i + 1] if i + 1 < len(rows) else rows[i]
            for i in range(0, len(rows), 2)
        ]
    return rows[0]


def order_kernel(nbr2, nbr1, mid_self, out, slots, info, ordered, copied):
    copies = [
        pltpu.make_async_copy(nbr2.at[k, 0], slots.at[pl.ds(k * SEEDS, SEEDS)], copied.at[k])
        for k in range(FAN1)
    ]
    for copy in copies:
        copy.start()
    empty = jnp.zeros((128 - POSITIONS, 128), jnp.int32)

    def by_node(i, carry):
        at = pl.ds(pl.multiple_of(i * 128, 128), 128)
        rows = [nbr1[k, :, at] for k in range(FAN0)] + [mid_self[:, at]]
        info[at, :] = jnp.concatenate([*rows, empty], axis=0).T
        return carry

    lax.fori_loop(0, MID // 128, by_node, 0, unroll=10)
    for k in range(FAN0):
        out[k, :, 0:SEEDS] = nbr1[k, :, 0:SEEDS]
    out[FAN0, :, 0:SEEDS] = mid_self[:, 0:SEEDS]
    for copy in copies:
        copy.wait()

    chunks = MID // 128

    def by_chunk(i, carry):
        before = jnp.maximum(i - 1, 0) * 128
        rows = ordered[pl.ds(pl.multiple_of(before, 128), 128), :].T
        base = jnp.minimum(i, chunks - 1) * 128
        for u in range(128):
            ordered[pl.ds(base + u, 1), :] = info[pl.ds(slots[base + u], 1), :]
        at = pl.ds(pl.multiple_of(SEEDS + before, 128), 128)
        for k in range(POSITIONS):
            out[k, :, at] = rows[k : k + 1, :]
        return carry

    lax.fori_loop(0, chunks + 1, by_chunk, 0)


def order_positions(nbr1, nbr2, mid_self):
    vmem = pl.BlockSpec(memory_space=pltpu.VMEM)
    return pl.pallas_call(
        order_kernel,
        out_shape=jax.ShapeDtypeStruct((POSITIONS, 1, SLOTS), jnp.int32),
        in_specs=[pl.BlockSpec(memory_space=pl.ANY), vmem, vmem],
        out_specs=vmem,
        scratch_shapes=[
            pltpu.SMEM((MID,), jnp.int32),
            pltpu.VMEM((MID, 128), jnp.int32),
            pltpu.VMEM((MID, 128), jnp.int32),
            pltpu.SemaphoreType.DMA((FAN1,)),
        ],
        compiler_params=pltpu.CompilerParams(vmem_limit_bytes=16 << 20),
        cost_estimate=pl.CostEstimate(flops=0, bytes_accessed=8 << 20, transcendentals=0),
        name="order",
    )(nbr2[:, None], nbr1[:, None], mid_self[None])


def train_kernel(
    counts, where_hot, core, places,
    hot0, hot1, hot2, hot3, cold, labels, w1_self, w1_neigh, w2_self, w2_neigh,
    loss_out, keep_out, send_out,
    n0, n1, n2, n3, n4, n5, n6, n7, n8, n9, own, copied,
    table, x_even, x_odd, w1, w2s, w2n, x_all, slope, hidden, hidden_b, grad_logits, back, w1_acc, terms,
):
    f32, bf16 = jnp.float32, jnp.bfloat16
    neighbours = (n0, n1, n2, n3, n4, n5, n6, n7, n8, n9)
    pieces = []
    for p, (start, stop) in enumerate(zip(PIECES[:-1], PIECES[1:])):
        at = pl.ds(start, stop - start)
        pieces.append(
            [
                pltpu.make_async_copy(places.at[k, 0, at], to.at[at], copied.at[p, k])
                for k, to in enumerate((*neighbours, own))
            ]
        )
    for copies in pieces:
        for copy in copies:
            copy.start()

    for d, block in enumerate((hot0, hot1, hot2, hot3)):
        start = pl.multiple_of(where_hot[d] * 512, 512)
        table[pl.ds(start, 512), :] = block[...].astype(f32)
    slot_index = lax.broadcasted_iota(jnp.int32, (32, F), 0)

    def place_cold(o, carry):
        rows = cold[o].astype(f32)
        live = slot_index < counts[o]
        table[pl.ds(pl.multiple_of(HOT_ROWS + o * 32, 32), 32), :] = jnp.where(live, rows, 0.0)
        return carry

    lax.fori_loop(0, 64, place_cold, 0, unroll=4)

    w1[0:F, :] = w1_self[...]
    w1[F : 2 * F, :] = w1_neigh[...]
    for padded, given in ((w2s, w2_self), (w2n, w2_neigh)):
        padded[...] = jnp.zeros((256, HID), bf16)
        padded[0:CLASSES, :] = given[...]
    hidden[...] = jnp.zeros((2 * SEEDS, HID), f32)

    def gather(chunk, buffer, part):
        base = chunk * STEP
        for u in part:
            m = base + u
            rows = [table[pl.ds(near[m], 1), :] for near in neighbours]
            buffer[u : u + 1, 0:F] = table[pl.ds(own[m], 1), :]
            buffer[u : u + 1, F : 2 * F] = tree_sum(rows)

    def forward(chunk, buffer):
        row = pl.multiple_of(chunk * STEP, STEP)
        x_all[pl.ds(row, STEP), 0:F] = buffer[:, 0:F].astype(bf16)
        x_all[pl.ds(row, STEP), F : 2 * F] = (buffer[:, F : 2 * F] * (1.0 / FAN0)).astype(bf16)
        x = jnp.concatenate(
            [buffer[:, 0:F].astype(bf16), (buffer[:, F : 2 * F] * (1.0 / FAN0)).astype(bf16)], axis=1
        )
        v = jnp.dot(x, w1[...], preferred_element_type=f32)
        square = v * v
        t = jnp.tanh(v * (GELU_C + (GELU_C * GELU_A) * square))
        half = 0.5 + 0.5 * t
        h = (v * half).astype(bf16).astype(f32)
        slope[pl.ds(row, STEP), :] = half + (0.5 * v) * (1.0 - t * t) * (
            GELU_C + (3.0 * GELU_C * GELU_A) * square
        )
        into = pl.multiple_of(
            lax.rem(chunk, SEED_CHUNKS) * STEP + jnp.where(chunk >= SEED_CHUNKS, SEEDS, 0), STEP
        )
        hidden[pl.ds(into, STEP), :] += h

    for copy in pieces[0]:
        copy.wait()
    gather(0, x_even, range(STEP))

    def two_chunks(i, carry):
        gather(2 * i + 1, x_odd, FIRST)
        forward(2 * i, x_even)
        gather(2 * i + 1, x_odd, SECOND)
        for p, start in enumerate(PIECES[1:-1]):

            @pl.when(2 * i + 2 == start // STEP)
            def _():
                for copy in pieces[p + 1]:
                    copy.wait()

        gather(lax.rem(2 * i + 2, CHUNKS), x_even, FIRST)
        forward(2 * i + 1, x_odd)
        gather(lax.rem(2 * i + 2, CHUNKS), x_even, SECOND)
        return carry

    lax.fori_loop(0, CHUNKS // 2, two_chunks, 0)

    hidden_b[0:SEEDS, :] = hidden[0:SEEDS, :].astype(bf16)
    hidden_b[SEEDS:, :] = (hidden[SEEDS:, :] / FAN1).astype(bf16)
    nt = (((1,), (1,)), ((), ()))
    tn = (((0,), (0,)), ((), ()))
    eye = lax.broadcasted_iota(jnp.int32, (128, 128), 0) == lax.broadcasted_iota(
        jnp.int32, (128, 128), 1
    )
    lane = lax.broadcasted_iota(jnp.int32, (128, 256), 1)
    for b in range(SEEDS // 128):
        rows = slice(b * 128, (b + 1) * 128)
        logits = lax.dot_general(
            hidden_b[rows, :], w2s[...], nt, preferred_element_type=f32
        ) + lax.dot_general(
            hidden_b[SEEDS + b * 128 : SEEDS + (b + 1) * 128, :], w2n[...], nt,
            preferred_element_type=f32,
        )
        label_row = labels[:, rows].astype(f32)
        label = jnp.sum(jnp.where(eye, label_row, 0.0), axis=1, keepdims=True).astype(jnp.int32)
        valid = lane < CLASSES
        top = jnp.max(jnp.where(valid, logits, -3.0e38), axis=1, keepdims=True)
        total = jnp.sum(jnp.where(valid, jnp.exp(logits - top), 0.0), axis=1, keepdims=True)
        log_total = jnp.log(total) + top
        hit = lane == label
        picked = jnp.sum(jnp.where(hit, logits, 0.0), axis=1, keepdims=True)
        loss = log_total - picked
        loss_out[:, rows] = jnp.sum(jnp.where(eye, loss, 0.0), axis=0, keepdims=True)
        probs = jnp.where(valid, jnp.exp(logits - log_total), 0.0)
        grad_logits[rows, :] = ((probs - hit.astype(f32)) / SEEDS).astype(bf16)

    left, right = core[0], 1 - core[0]
    g = grad_logits[...]
    terms[:, 608:, :] = jnp.zeros((2, HALF_ROWS - 608, F), f32)
    for at, part in ((256, slice(0, SEEDS)), (256 + CLASS_ROWS, slice(SEEDS, 2 * SEEDS))):
        term = lax.dot_general(g, hidden_b[part, :], tn, preferred_element_type=f32)
        terms[left, at : at + CLASS_ROWS, :] = term[0:CLASS_ROWS, 0:F]
        terms[right, at : at + CLASS_ROWS, :] = term[0:CLASS_ROWS, F:]
    back[0:SEEDS, :] = jnp.dot(g, w2s[...], preferred_element_type=f32)
    back[SEEDS:, :] = jnp.dot(g, w2n[...], preferred_element_type=f32) / FAN1

    def backward(j, into):
        row = pl.multiple_of(j * SEEDS, SEEDS)
        grad_pre = (slope[pl.ds(row, SEEDS), :] * back[into, :]).astype(bf16)
        return lax.dot_general(x_all[pl.ds(row, SEEDS), :], grad_pre, tn, preferred_element_type=f32)

    w1_acc[...] = backward(0, slice(0, SEEDS))

    def add_block(j, carry):
        terms_of = [backward(15 * j + 1 + i, slice(SEEDS, 2 * SEEDS)) for i in range(15)]
        w1_acc[...] += tree_sum(terms_of)
        return carry

    lax.fori_loop(0, FAN1 // 15, add_block, 0)
    terms[left, 0:256, :] = w1_acc[:, 0:F]
    terms[right, 0:256, :] = w1_acc[:, F:]
    keep_out[...] = terms[0]
    send_out[...] = terms[1]


def train(counts, where_hot, core, places, hot, cold, labels, w1_self, w1_neigh, w2_self_t, w2_neigh_t):
    smem = pl.BlockSpec(memory_space=pltpu.SMEM)
    vmem = pl.BlockSpec(memory_space=pltpu.VMEM)
    anywhere = pl.BlockSpec(memory_space=pl.ANY)
    return pl.pallas_call(
        train_kernel,
        out_shape=(
            jax.ShapeDtypeStruct((1, SEEDS), jnp.float32),
            jax.ShapeDtypeStruct((HALF_ROWS, F), jnp.float32),
            jax.ShapeDtypeStruct((HALF_ROWS, F), jnp.float32),
        ),
        in_specs=[smem] * 3 + [anywhere] + [vmem] * 10,
        out_specs=(vmem, vmem, vmem),
        scratch_shapes=[
            *[pltpu.SMEM((SLOTS,), jnp.int32) for _ in range(POSITIONS)],
            pltpu.SemaphoreType.DMA((len(PIECES) - 1, POSITIONS)),
            pltpu.VMEM((HOT_ROWS + COLD_ROWS, F), jnp.float32),
            pltpu.VMEM((STEP, 2 * F), jnp.float32),
            pltpu.VMEM((STEP, 2 * F), jnp.float32),
            pltpu.VMEM((2 * F, HID), jnp.bfloat16),
            pltpu.VMEM((256, HID), jnp.bfloat16),
            pltpu.VMEM((256, HID), jnp.bfloat16),
            pltpu.VMEM((SLOTS, 2 * F), jnp.bfloat16),
            pltpu.VMEM((SLOTS, HID), jnp.float32),
            pltpu.VMEM((2 * SEEDS, HID), jnp.float32),
            pltpu.VMEM((2 * SEEDS, HID), jnp.bfloat16),
            pltpu.VMEM((SEEDS, 256), jnp.bfloat16),
            pltpu.VMEM((2 * SEEDS, HID), jnp.float32),
            pltpu.VMEM((2 * F, HID), jnp.float32),
            pltpu.VMEM((2, HALF_ROWS, F), jnp.float32),
        ],
        compiler_params=pltpu.CompilerParams(vmem_limit_bytes=44 << 20),
        cost_estimate=pl.CostEstimate(flops=4 << 30, bytes_accessed=4 << 20, transcendentals=2 << 20),
        name="train",
    )(
        counts, where_hot, core, places, *hot, cold, labels, w1_self, w1_neigh, w2_self_t, w2_neigh_t,
    )


def pick_kernel(n, *refs):
    asked, shard, given = refs[:n], refs[n], refs[n + 1 : 2 * n + 1]
    wide, picked = refs[2 * n + 1 :]
    step = shard.shape[0] // PARTS
    for i in range(PARTS):
        part = pl.ds(i * step, step)
        wide[part, :] = shard[part, :].astype(jnp.float32)
    row = 0
    for ids, out in zip(asked, given):
        first = row
        for at in np.ndindex(ids.shape):
            picked[row : row + 1, :] = wide[pl.ds(ids[at], 1), :]
            row += 1
        if len(out.shape) == 2:
            out[...] = picked[first:row, :].astype(out.dtype)
        else:
            size = out.shape[1]
            for o in range(out.shape[0]):
                out[o] = picked[first + o * size : first + (o + 1) * size, :].astype(out.dtype)


def pick_rows(shard, asked, name):
    n = len(asked)
    total = sum(int(np.prod(ids.shape)) for ids in asked)
    return pl.pallas_call(
        lambda *refs: pick_kernel(n, *refs),
        out_shape=tuple(jax.ShapeDtypeStruct(ids.shape + (F,), jnp.bfloat16) for ids in asked),
        in_specs=[pl.BlockSpec(memory_space=pltpu.SMEM)] * n + [pl.BlockSpec(memory_space=pltpu.VMEM)],
        out_specs=tuple(pl.BlockSpec(memory_space=pltpu.VMEM) for _ in asked),
        scratch_shapes=[
            pltpu.VMEM(shard.shape, jnp.float32),
            pltpu.VMEM((total, F), jnp.float32),
        ],
        compiler_params=pltpu.CompilerParams(vmem_limit_bytes=24 << 20),
        cost_estimate=pl.CostEstimate(flops=0, bytes_accessed=4 << 20, transcendentals=0),
        name=name,
    )(*asked, shard)


def clique_peers(hot_ids):
    me = lax.axis_index("clique")
    peers = [lax.rem(me + d, 4) for d in range(4)]
    return peers, [lax.dynamic_index_in_dim(hot_ids, peer, 0, keepdims=False) for peer in peers]


def send_hot(rows):
    return [rows[0]] + [
        lax.ppermute(rows[d], "clique", [(i, (i - d) % 4) for i in range(4)]) for d in (1, 2, 3)
    ]


def exchange(x, axes):
    return lax.all_to_all(x, axes, split_axis=0, concat_axis=0, tiled=True)


def share(x, axes, n):
    return exchange(jnp.broadcast_to(x[None], (n,) + x.shape), axes)


SWAP = [(0, 1), (1, 0)]


def split_kernel(core, mine, other, *outs):
    for first, at in ((0, slice(0, F)), (1, slice(F, 2 * F))):
        for out, row in zip(outs, (0, F, 2 * F, 2 * F + CLASS_ROWS)):
            rows = slice(row, row + out.shape[0])
            out[:, at] = jnp.where(core[0] == first, mine[rows, :], other[rows, :])


def sum_everywhere(keep, send, core):
    mine = keep + lax.ppermute(send, "core", SWAP)
    mine = exchange(mine.reshape(16, HALF_ROWS // 128, 8, F), ("clique", "y")).sum(0)
    mine = share(mine, "z", 8).sum(0)
    mine = share(mine, ("clique", "y"), 16).reshape(HALF_ROWS, F)
    other = lax.ppermute(mine, "core", SWAP)
    vmem = pl.BlockSpec(memory_space=pltpu.VMEM)
    return pl.pallas_call(
        split_kernel,
        out_shape=tuple(jax.ShapeDtypeStruct((n, HID), jnp.float32) for n in (F, F, CLASSES, CLASSES)),
        in_specs=[pl.BlockSpec(memory_space=pltpu.SMEM), vmem, vmem],
        out_specs=(vmem,) * 4,
        compiler_params=pltpu.CompilerParams(vmem_limit_bytes=8 << 20),
        name="split",
    )(core, mine, other)


def body(
    hot_shard, cold_shard, hot_ids, cold_ids, cold_counts, mid_self, nbr1, nbr2, labels,
    w1_self, w1_neigh, w2_self, w2_neigh,
):
    peers, hot_asked = clique_peers(hot_ids[0])
    hot_asked[1:] = [
        lax.ppermute(hot_asked[d], "clique", [(i, (i + d) % 4) for i in range(4)]) for d in (1, 2, 3)
    ]
    cold_asked = exchange(cold_ids[0], GROUP)
    *hot_asked, cold_asked = lax.optimization_barrier((*hot_asked, cold_asked))
    (served,) = pick_rows(cold_shard, [cold_asked], "pick_cold")
    cold = exchange(served, GROUP)
    *hot_asked, served = lax.optimization_barrier((*hot_asked, served))
    rows = pick_rows(hot_shard, hot_asked, "pick_hot")
    *rows, nbr2 = lax.optimization_barrier((*rows, nbr2))
    hot = send_hot(rows)
    places = order_positions(nbr1[0], nbr2[0], mid_self[0])
    core = lax.axis_index("core").astype(jnp.int32)[None]
    loss, keep, send = train(
        cold_counts[0], jnp.stack(peers).astype(jnp.int32), core, places,
        hot, cold, labels, w1_self, w1_neigh, w2_self.T, w2_neigh.T,
    )
    w1s, w1n, w2s, w2n = sum_everywhere(keep, send, core)
    return loss, w1s, w1n, w2s.T, w2n.T


def solution(mesh):
    mesh = Mesh(mesh.devices.reshape(4, 8, 4, 2), AXES)
    each = P(AXES)
    return jax.shard_map(
        body,
        mesh=mesh,
        in_specs=(P("clique"), P(GROUP)) + (each,) * 7 + (P(),) * 4,
        out_specs=(each, P(), P(), P(), P()),
        check_vma=False,
    )
```
